128 devices in a mesh: sample: 32 (over z_hi, y, x), prompt: 2 (over z_lo), tensor: 2 (over core).
Axes of the slice: x: 4, y: 4, z: 4 (z_hi: 2, z_lo: 2; z = z_hi * 2 + z_lo), core: 2. Of those that a mesh axis runs over, the one named last changes fastest.
Arguments:
- hidden_input: bfloat16 [4, 96, 8192], P(None, 'prompt'), parts along dimension 1, may hold values from -6 to 6
- prompt_lengths: int32 [6], P('prompt'), parts along dimension 0, may hold values from 1 to 1024, 1920 in all
- prompt_states: float32 [6, 256, 64, 256], P('prompt', None, None, ('sample', 'tensor')), parts along dimension 0, may hold values from -0.8 to 0.8
- prompt_cache: bfloat16 [6, 1024, 8, 256], P('prompt', ('sample', 'tensor')), parts along dimension 0, may hold values from -6 to 6
- input_gain: float32 [8192], replicated, may hold values from 0.25 to 1.75
- gate_weight: bfloat16 [8192, 16384], P(None, ('sample', 'tensor')), may hold values from -0.0625 to 0.0625
- input_weight: bfloat16 [8192, 16384], P(None, ('sample', 'tensor')), may hold values from -0.0625 to 0.0625
- rate_weight: bfloat16 [8192, 256], P(None, ('sample', 'tensor')), may hold values from -0.0625 to 0.0625
- rate_bias: float32 [256], P(('sample', 'tensor')), may hold values from -3 to 1
- decay_log: float32 [256], P(('sample', 'tensor')), may hold values from -2 to 2
- skip_gain: float32 [256], P(('sample', 'tensor')), may hold values from 0.5 to 2
- state_io_weight: bfloat16 [8192, 4096], P(('sample', 'tensor')), may hold values from -0.0625 to 0.0625
- mix_gain: float32 [16384], P(('sample', 'tensor')), may hold values from 0.25 to 1.75
- mix_weight: bfloat16 [16384, 8192], P(('sample', 'tensor')), may hold values from -0.046875 to 0.046875
- middle_gain: float32 [8192], replicated, may hold values from 0.25 to 1.75
- query_weight: bfloat16 [8192, 8192], P(None, ('sample', 'tensor')), may hold values from -0.0625 to 0.0625
- key_value_weight: bfloat16 [8192, 2048], P(('sample', 'tensor')), may hold values from -0.0625 to 0.0625
- output_weight: bfloat16 [8192, 8192], P(('sample', 'tensor')), may hold values from -0.0625 to 0.0625
Outputs:
- layer_out: bfloat16 [384, 8192], P(('prompt', 'sample', 'tensor')), parts along dimension 0
The draws below stay inside these ranges and needn't reach their ends.
There are 2 independent parts, one for each index of `prompt`. The reference program is written for one: setup_inputs(seed, part) draws one part's arguments, and reference() takes and returns one part's arrays. A program takes and returns all parts, laid end to end along the dimension named above; an argument that names none is the same for every part. Nothing has to cross between parts.
Inputs may be any that keep to these rules, and one draw needn't show every extreme that they name: `prompt_lengths`: every prompt has at least one valid position; the longest prompt fills all 1024 positions.
All inputs are finite; a program needn't handle non-finite values.
Results may differ from the reference program's by a relative error of at most 0.009.
The reference program's roundings to bfloat16 on the way count: a program that leaves them out, or rounds other values in their place, can miss the bound.
Values may be sent and summed in bfloat16 or wider, within the bound.
A program may use at most 128 MiB of HBM per device.

```python
import math
import jax
import jax.numpy as jnp
import numpy as np
from jax import lax

D = 8192
HD = 64
NS = 256
NG = 8
KVH = 8
HDA = 128
SAMPLES = 16
STEPS = 4
PROMPTS = 3
LEN = 1024
MH = 256
QH = 64
GS = 2048
ROWS = 48
TOKENS = 192


def block_scale(own_key, extent, cuts, low, top_value):
    def one(dim, shards_of):
        heights = jax.random.uniform(jax.random.fold_in(jax.random.fold_in(own_key, 6), dim), (shards_of,), jnp.float32, low / len(cuts), top_value / len(cuts))
        return jnp.repeat(jnp.exp(heights), extent[dim] // shards_of).reshape((-1,) + (1,) * (len(extent) - dim - 1))

    factor_of = one(*cuts[0])
    for cut in cuts[1:]:
        factor_of = factor_of * one(*cut)
    return factor_of


def split_up(amount, total, most, lean):
    portions = [(1 << 20) // math.isqrt(rank ** lean) + 1 for rank in range(2, amount + 1)]
    spare, counts = total - most - (amount - 1), [1] * (amount - 1)
    while spare > 0:
        movable = [i for i in range(amount - 1) if counts[i] < most]
        whole, left = sum([portions[i] for i in movable]), spare
        for i in movable:
            addition = min(most - counts[i], max(1, left * portions[i] // whole), spare)
            counts[i] = counts[i] + addition
            spare = spare - addition
    return np.array([most] + counts)


def uneven_parts(own_key, amount, total, reach, lean):
    if amount == 2:
        one = jax.random.randint(own_key, (), max(1, total - reach), min(reach, total - 1) + 1)
        return jnp.stack([one, total - one])
    lengths = jnp.asarray(split_up(amount, total, reach, lean), jnp.int32)
    couples = (amount - 1) // 2
    source_of, sink = lengths[1:1 + 2 * couples:2], lengths[2:2 + 2 * couples:2]
    slack = jnp.minimum(source_of - 1, reach - sink)
    passed = jax.random.randint(jax.random.fold_in(own_key, 1), (couples,), 0, 1 << 20) % (slack + 1)
    lengths = lengths.at[1:1 + 2 * couples:2].set(source_of - passed).at[2:2 + 2 * couples:2].set(sink + passed)
    return lengths[jax.random.permutation(jax.random.fold_in(own_key, 2), amount)]


def centred(key, shape, scale, reach, shards=(), dtype=jnp.bfloat16):
    gain = block_scale(key, shape, shards, -0.22, 0.18) if shards else 1.0
    array = jax.random.normal(key, shape, jnp.float32) * scale * gain
    return jnp.minimum(jnp.maximum(array, -reach), reach).astype(dtype)


def setup_inputs(seed: int = 0, part: int = 0) -> dict:
    key_of = jax.random.split(jax.random.key(seed), 19)
    part_splits = jax.random.split(jax.random.fold_in(key_of[18], part), 19)
    hidden_input = centred(part_splits[0], (STEPS, ROWS, D), 1.0, 6.0)
    prompt_lengths = uneven_parts(part_splits[1], PROMPTS, PROMPTS * LEN * 5 // 8, LEN, 1).astype(jnp.int32)
    prompt_states = centred(part_splits[2], (PROMPTS, MH, HD, NS), 0.1, 0.8, ((3, 64),), jnp.float32)
    prompt_cache = centred(part_splits[3], (PROMPTS, LEN, KVH, 2 * HDA), 1.0, 6.0, ((1, 64),))
    input_gain = jnp.clip(1.0 + 0.15 * jax.random.normal(key_of[4], (D,), jnp.float32), 0.25, 1.75)
    gate_weight = centred(key_of[5], (D, MH * HD), D ** -0.5, 0.0625, ((1, 64),))
    input_weight = centred(key_of[6], (D, MH * HD), D ** -0.5, 0.0625, ((1, 64),))
    rate_weight = centred(key_of[7], (D, MH), D ** -0.5, 0.0625, ((1, 64),))
    rate_bias = jnp.clip(-3.0 + 4.0 * jax.random.uniform(key_of[8], (MH,), jnp.float32) ** block_scale(key_of[8], (MH,), ((0, 64),), -0.2, 0.2), -3.0, 1.0)
    decay_log = jnp.clip(jax.random.uniform(key_of[9], (MH,), jnp.float32, -2.0, 2.0) * block_scale(key_of[9], (MH,), ((0, 64),), -0.4, 0.0), -2.0, 2.0)
    skip_gain = jnp.clip(0.5 + 1.5 * jax.random.uniform(key_of[10], (MH,), jnp.float32) ** block_scale(key_of[10], (MH,), ((0, 64),), -0.2, 0.2), 0.5, 2.0)
    state_io_weight = centred(key_of[11], (D, NG * 2 * NS), D ** -0.5, 0.0625, ((0, 64),))
    mix_gain = jnp.clip(1.0 + 0.15 * jax.random.normal(key_of[12], (MH * HD,), jnp.float32), 0.25, 1.75)
    mix_weight = centred(key_of[13], (MH * HD, D), (MH * HD) ** -0.5, 0.046875, ((0, 64),))
    middle_gain = jnp.clip(1.0 + 0.15 * jax.random.normal(key_of[14], (D,), jnp.float32), 0.25, 1.75)
    query_weight = centred(key_of[15], (D, QH * HDA), D ** -0.5, 0.0625, ((1, 64),))
    key_value_weight = centred(key_of[16], (D, KVH * 2 * HDA), D ** -0.5, 0.0625, ((0, 64),))
    output_weight = centred(key_of[17], (QH * HDA, D), (QH * HDA) ** -0.5, 0.0625, ((0, 64),))
    return {"hidden_input": hidden_input, "prompt_lengths": prompt_lengths, "prompt_states": prompt_states, "prompt_cache": prompt_cache, "input_gain": input_gain, "gate_weight": gate_weight, "input_weight": input_weight, "rate_weight": rate_weight, "rate_bias": rate_bias, "decay_log": decay_log, "skip_gain": skip_gain, "state_io_weight": state_io_weight, "mix_gain": mix_gain, "mix_weight": mix_weight, "middle_gain": middle_gain, "query_weight": query_weight, "key_value_weight": key_value_weight, "output_weight": output_weight}


def normalize(values, gain_row):
    scale = lax.rsqrt(lax.optimization_barrier(jnp.mean(values * values, axis=-1, keepdims=True)) + 1e-05)
    return values * scale * gain_row

def round_bf16(values):
    return lax.optimization_barrier(values.astype(jnp.bfloat16)).astype(jnp.float32)

def group_scan(pieces):
    inner_part, rate_part, decay_part, io_part, start_part, skip_part = pieces
    carried = jnp.repeat(start_part, SAMPLES, axis=0)
    results = []
    for moment in range(STEPS):
        entering = rate_part[moment][:, :, None] * inner_part[moment]
        carried = decay_part[moment][:, :, None, None] * carried + entering[:, :, :, None] * io_part[moment][:, None, None, :NS]
        readout = jnp.einsum('rhdn,rn->rhd', carried, io_part[moment][:, NS:], precision=lax.Precision.HIGHEST)
        results.append(readout + skip_part[None, :, None] * inner_part[moment])
    return jnp.stack(results)

def reference(hidden_input, prompt_lengths, prompt_states, prompt_cache, input_gain, gate_weight, input_weight, rate_weight, rate_bias, decay_log, skip_gain, state_io_weight, mix_gain, mix_weight, middle_gain, query_weight, key_value_weight, output_weight):
    per_group = MH // NG
    flat_rows = hidden_input.reshape(TOKENS, D).astype(jnp.float32)
    normed = normalize(flat_rows, input_gain).astype(jnp.bfloat16)
    gate_proj = jnp.dot(normed, gate_weight, preferred_element_type=jnp.float32)
    inner_proj = jnp.dot(normed, input_weight, preferred_element_type=jnp.float32)
    step_rate = jax.nn.softplus(jnp.dot(normed, rate_weight, preferred_element_type=jnp.float32) + rate_bias)
    decay_rate = jnp.exp(step_rate * -jnp.exp(decay_log))
    state_io = round_bf16(jnp.dot(normed, state_io_weight, preferred_element_type=jnp.float32))
    inner_groups = jnp.moveaxis(inner_proj.reshape(STEPS, ROWS, NG, per_group, HD), 2, 0)
    rate_groups = jnp.moveaxis(step_rate.reshape(STEPS, ROWS, NG, per_group), 2, 0)
    decay_groups = jnp.moveaxis(decay_rate.reshape(STEPS, ROWS, NG, per_group), 2, 0)
    io_groups = jnp.moveaxis(state_io.reshape(STEPS, ROWS, NG, 2 * NS), 2, 0)
    start_groups = jnp.moveaxis(prompt_states.reshape(PROMPTS, NG, per_group, HD, NS), 1, 0)
    skip_groups = skip_gain.reshape(NG, per_group)
    scanned = lax.map(group_scan, (inner_groups, rate_groups, decay_groups, io_groups, start_groups, skip_groups))
    mixed_out = jnp.moveaxis(scanned, 0, 2).reshape(TOKENS, MH * HD)
    gated_out = (mixed_out * jax.nn.silu(gate_proj)).reshape(TOKENS, NG, GS)
    inverse = lax.rsqrt(lax.optimization_barrier(jnp.mean(gated_out * gated_out, axis=-1, keepdims=True)) + 1e-05)
    scaled = ((gated_out * inverse).reshape(TOKENS, MH * HD) * mix_gain).astype(jnp.bfloat16)
    residual = flat_rows + jnp.dot(scaled, mix_weight, preferred_element_type=jnp.float32)
    middle = normalize(residual, middle_gain).astype(jnp.bfloat16)
    query_rows = (jnp.dot(middle, query_weight, preferred_element_type=jnp.float32) * HDA ** (-0.5)).astype(jnp.bfloat16)
    pair_rows = jnp.dot(middle, key_value_weight, preferred_element_type=jnp.float32).astype(jnp.bfloat16)
    head_map = (jnp.arange(QH) * KVH // QH).astype(jnp.int32)
    query_heads = jnp.moveaxis(query_rows.reshape(STEPS, ROWS, QH, HDA), 2, 0).astype(jnp.float32)
    pair_heads = jnp.moveaxis(pair_rows.reshape(STEPS, ROWS, KVH, 2 * HDA), 2, 0)[head_map].astype(jnp.float32)
    valid_mask = jnp.repeat(jnp.arange(LEN)[None, :] < prompt_lengths[:, None], SAMPLES, axis=0)
    causal = jnp.arange(STEPS)[:, None] >= jnp.arange(STEPS)[None, :]

    def head_attention(pieces):
        query_part, pair_part, cache_index = pieces
        cache_part = lax.dynamic_index_in_dim(prompt_cache, cache_index, axis=2, keepdims=False).astype(jnp.float32)
        query_grid = query_part.reshape(STEPS, PROMPTS, SAMPLES, HDA)
        far_scores = jnp.einsum('tpsd,pld->tpsl', query_grid, cache_part[:, :, :HDA]).reshape(STEPS, ROWS, LEN)
        far_scores = jnp.where(valid_mask[None], far_scores, -1e+30)
        near_scores = jnp.einsum('trd,urd->tru', query_part, pair_part[:, :, :HDA])
        near_scores = jnp.where(causal[:, None, :], near_scores, -1e+30)
        row_top = jnp.maximum(lax.optimization_barrier(jnp.max(far_scores, axis=-1)), lax.optimization_barrier(jnp.max(near_scores, axis=-1)))
        far_exp = jnp.exp(far_scores - row_top[..., None])
        near_exp = jnp.exp(near_scores - row_top[..., None])
        row_total = lax.optimization_barrier(jnp.sum(far_exp, axis=-1)) + lax.optimization_barrier(jnp.sum(near_exp, axis=-1))
        far_weight = round_bf16(far_exp / row_total[..., None])
        near_weight = round_bf16(near_exp / row_total[..., None])
        far_part = jnp.einsum('tpsl,pld->tpsd', far_weight.reshape(STEPS, PROMPTS, SAMPLES, LEN), cache_part[:, :, HDA:])
        near_part = jnp.einsum('tru,urd->trd', near_weight, pair_part[:, :, HDA:])
        return (far_part.reshape(STEPS, ROWS, HDA) + near_part).astype(jnp.bfloat16)
    attended = lax.map(head_attention, (query_heads, pair_heads, head_map))
    attended = jnp.moveaxis(attended, 0, 2).reshape(TOKENS, QH * HDA)
    result = residual + jnp.dot(attended, output_weight, preferred_element_type=jnp.float32)
    return result.astype(jnp.bfloat16)
```

```python
import jax
import jax.numpy as jnp
from jax import lax
from jax.experimental import pallas as pl
from jax.experimental.pallas import tpu as pltpu
from jax.sharding import PartitionSpec as P

F32 = jnp.float32
BF16 = jnp.bfloat16
MESH = pl.DeviceIdType.MESH
HIGH = lax.Precision.HIGHEST

STAGES = (
    "wio",
    "st1",
    "kvw",
    "ca1",
    "st2",
    "ca2",
    "iors",
    "ioag",
    "sq",
    "gm",
    "a1",
    "b1",
    "a2",
    "b2",
    "rz",
    "sq2",
    "sqy",
    "ma1",
    "mb1",
    "ma2",
    "mb2",
    "q",
    "kvr",
    "kva",
    "at",
    "c1",
    "d1",
    "c2",
    "d2",
    "sz",
    "fin",
    "w",
    "loc",
    "pro",
    "a1x",
    "b1x",
    "a2x",
    "b2x",
    "ma1x",
    "mb1x",
    "ma2x",
    "mb2x",
    "c1x",
    "d1x",
    "c2x",
    "d2x",
)
STAGE = {name: number for number, name in enumerate(STAGES)}


def nt_dot(left, right, precision=None):
    return lax.dot_general(
        left, right, (((1,), (1,)), ((), ())), preferred_element_type=F32, precision=precision
    )


def row_sums(values):
    ones = jnp.ones((8, values.shape[1]), F32)
    return nt_dot(ones, values * values, HIGH)


def to_column(rows):
    size = rows.shape[1]
    eye = (
        lax.broadcasted_iota(jnp.int32, (size, size), 0)
        == lax.broadcasted_iota(jnp.int32, (size, size), 1)
    ).astype(F32)
    return nt_dot(eye, rows, HIGH)[:, :1]


def kernel(
    lens,
    hid_h,
    st_h,
    cache_h,
    gain1,
    wg_h,
    wi_h,
    wrt,
    rate_bias,
    decay_log,
    skip_gain,
    mix_gain,
    wio_h,
    wm_h,
    gain2,
    wq_h,
    wkv_h,
    wo_h,
    out,
    hid,
    nrm,
    wg,
    wi,
    wm,
    wq,
    wo,
    wio,
    kvw,
    st1,
    st2,
    ca1,
    ca2,
    accg,
    acci,
    accr,
    nio,
    iop,
    ior,
    iog,
    sq,
    gm,
    part,
    ra1,
    rb1,
    qa,
    qb,
    ra2,
    rb2,
    rzs,
    rzr,
    res,
    sq2,
    sqy,
    mid,
    qs,
    qr,
    kvp,
    kvr,
    kvg,
    scores,
    os,
    orr,
    att,
    part2,
    rc1,
    rd1,
    qc,
    qd,
    rc2,
    rd2,
    szs,
    szr,
    fin,
    fo,
    fi,
    ssem,
    rsem,
):
    s = lax.axis_index("sample")
    t = lax.axis_index("tensor")
    z = lax.div(s, 16)
    y = lax.rem(lax.div(s, 4), 4)
    x = lax.rem(s, 4)
    g = lax.div(s, 4)
    i = 2 * x + t

    def al(value, size):
        return pl.multiple_of(value, size)

    def dev(sample, tensor):
        return {"sample": sample, "tensor": tensor}

    def dev_big_x(j):
        return dev(4 * g + lax.div(j, 2), lax.rem(j, 2))

    def dev_big_y(j):
        return dev(4 * j + x, t)

    def dev_x(j):
        return dev(4 * g + j, t)

    def dev_y(j):
        return dev(16 * z + 4 * j + x, t)

    sibling = dev(s, 1 - t)
    zpeer = dev(16 * (1 - z) + 4 * y + x, t)

    def remote(src, dst, stage, send_slot, recv_slot, device):
        return pltpu.make_async_remote_copy(
            src_ref=src,
            dst_ref=dst,
            send_sem=ssem.at[STAGE[stage], send_slot],
            recv_sem=rsem.at[STAGE[stage], recv_slot],
            device_id=device,
            device_id_type=MESH,
        )

    def local(src, dst, stage, slot):
        return pltpu.make_async_copy(src, dst, rsem.at[STAGE[stage], slot])

    pending = {}
    finish = []

    def exchange(stage, size, me, device, src_of, dst_of, own=False):
        def send(k, _):
            j = lax.rem(me + k, size)
            remote(src_of(j), dst_of(me), stage, j, me, device(j)).start()
            return 0

        def received(k, _):
            j = lax.rem(me + k, size)
            local(dst_of(j), dst_of(j), stage, j).wait()
            return 0

        def sent(k, _):
            j = lax.rem(me + k, size)
            pltpu.make_async_copy(src_of(j), src_of(j), ssem.at[STAGE[stage], j]).wait()
            return 0

        if own:
            local(src_of(me), dst_of(me), stage, me).start()
        lax.fori_loop(1, size, send, 0)
        pending[stage] = lambda: lax.fori_loop(0 if own else 1, size, received, 0)
        finish.append(lambda: lax.fori_loop(1, size, sent, 0))

    def swap(stage, src, dst, device, slot=0):
        copy = remote(src, dst, stage, slot, slot, device)
        copy.start()
        pending[stage, slot] = copy.wait_recv
        finish.append(copy.wait_send)

    def fetch(stage, src, dst, slot):
        copy = local(src, dst, stage, slot)
        copy.start()
        pending[stage, slot] = copy.wait

    def arrive(*names):
        for name in names:
            pending.pop(name)()

    def drain():
        for name in list(pending):
            arrive(name)
        for wait in finish:
            wait()

    fetch("loc", hid_h, hid, 0)

    def proj_copy(c, src, dst, slot):
        rows = pl.ds(al(c * 1024, 1024), 1024)
        return local(src.at[rows], dst.at[rows], "pro", 2 * c + slot)

    def start_proj(c, _):
        proj_copy(c, wg_h, wg, 0).start()
        proj_copy(c, wi_h, wi, 1).start()
        return 0

    lax.fori_loop(0, 8, start_proj, 0)

    def project_wait(c, _):
        proj_copy(c, wg_h, wg, 0).wait()
        proj_copy(c, wi_h, wi, 1).wait()
        return 0

    pending["pro"] = lambda: lax.fori_loop(0, 8, project_wait, 0)

    barrier = pltpu.get_barrier_semaphore()
    me = 2 * s + t

    def greet(k, _):
        j = lax.rem(me + k, 64)
        pl.semaphore_signal(
            barrier, inc=1, device_id=dev(lax.div(j, 2), lax.rem(j, 2)), device_id_type=MESH
        )
        return 0

    lax.fori_loop(1, 64, greet, 0)
    pl.semaphore_wait(barrier, 63)

    def wio_src(j):
        return wio_h.at[:, pl.ds(al(512 * j, 512), 512)]

    exchange("ca1", 8, g, dev_big_y, lambda j: cache_h.at[j], lambda j: ca1.at[:, j], own=True)
    exchange("st1", 8, i, dev_big_x, lambda j: st_h.at[j], lambda j: st1.at[j], own=True)
    exchange("wio", 8, g, dev_big_y, wio_src, lambda j: wio.at[j], own=True)

    half = al(4096 * t, 4096)
    other = al(4096 * (1 - t), 4096)
    own_rows = pl.ds(al(256 * t, 256), 256)
    head_rows = pl.ds(al(128 * t, 128), 128)
    fetch("loc", wm_h.at[:, pl.ds(half, 4096)], wm.at[own_rows], 1)
    swap("w", wm_h.at[:, pl.ds(other, 4096)], wm.at[own_rows], sibling, 0)
    fetch("loc", wq_h.at[pl.ds(half, 4096)], wq.at[:, head_rows], 2)
    swap("w", wq_h.at[pl.ds(other, 4096)], wq.at[:, head_rows], sibling, 1)
    fetch("loc", wo_h.at[:, pl.ds(half, 4096)], wo.at[head_rows], 3)
    swap("w", wo_h.at[:, pl.ds(other, 4096)], wo.at[head_rows], sibling, 2)

    arrive(("loc", 0))

    def norm_rows(r, _):
        rows = pl.ds(al(16 * r, 16), 16)
        values = hid[rows, :].astype(F32)
        scale = lax.rsqrt(jnp.mean(values * values, axis=1, keepdims=True) + 1e-05)
        nrm[rows, :] = (values * scale * gain1[...]).astype(BF16)
        return 0

    lax.fori_loop(0, 12, norm_rows, 0)
    arrive("ca1")
    exchange("ca2", 4, x, dev_x, lambda j: ca1, lambda j: ca2.at[j], own=True)

    accg[...] = jnp.zeros_like(accg)
    acci[...] = jnp.zeros_like(acci)
    accr[...] = jnp.zeros_like(accr)

    pending.pop("pro")

    def project(c, _):
        project_wait(c, 0)
        span = pl.ds(al(c * 1024, 1024), 1024)
        left = nrm[:, span]
        accg[...] += jnp.dot(left, wg[span, :], preferred_element_type=F32)
        acci[...] += jnp.dot(left, wi[span, :], preferred_element_type=F32)
        accr[...] += nt_dot(left, wrt[:, span])
        return 0

    lax.fori_loop(0, 8, project, 0)

    def pick(c, _):
        nio[:, pl.ds(al(128 * c, 128), 128)] = nrm[:, pl.ds(al(128 * (8 * c + i), 128), 128)]
        return 0

    lax.fori_loop(0, 8, pick, 0)
    arrive("wio", "st1")
    exchange("st2", 8, g, dev_big_y, lambda j: st1.at[:, j], lambda j: st2.at[j], own=True)
    io_part = jnp.dot(nio[...], wio[...].reshape(1024, 512), preferred_element_type=F32)
    for j in range(8):
        iop[j] = io_part[24 * j : 24 * j + 24]
    exchange("iors", 8, i, dev_big_x, lambda j: iop.at[j], lambda j: ior.at[j])
    arrive("iors")
    io_sum = iop[i]
    for k in range(1, 8):
        io_sum = io_sum + ior[lax.rem(i + k, 8)]
    iog[i] = io_sum.astype(BF16)
    exchange("ioag", 8, i, dev_big_x, lambda j: iog.at[i], lambda j: iog.at[j])

    lift = (
        lax.broadcasted_iota(jnp.int32, (4, 256), 0)
        == lax.div(lax.broadcasted_iota(jnp.int32, (4, 256), 1), 64)
    ).astype(F32)

    def widen(heads):
        return jnp.dot(heads, lift, preferred_element_type=F32, precision=HIGH)

    raw = widen(accr[...] + rate_bias[...])
    rate = jnp.maximum(raw, 0.0) + jnp.log1p(jnp.exp(-jnp.abs(raw)))
    decay = jnp.exp(rate * -jnp.exp(widen(decay_log[...])))
    skip = widen(skip_gain[...])
    entering = rate * acci[...]
    column = lax.broadcasted_iota(jnp.int32, (256, 1024), 1)
    inside = lax.rem(column, 16)
    owner = lax.div(column, 16)
    spread = (
        (4 * owner + lax.rem(inside, 4) == lax.broadcasted_iota(jnp.int32, (256, 1024), 0))
        & (inside < 12)
    )
    spread = jnp.where(spread, 1.0, 0.0).astype(BF16)

    arrive("ioag")
    def kvw_src(j):
        return wkv_h.at[:, pl.ds(al(256 * j, 256), 256)]

    kvw_slot = 2 * y + t

    def kvw_copy(j):
        return remote(kvw_src(j), kvw.at[kvw_slot], "kvw", j, kvw_slot, dev(4 * j + x, z))

    def kvw_send(k, _):
        kvw_copy(lax.rem(g + k, 8)).start()
        return 0

    lax.fori_loop(1, 8, kvw_send, 0)

    @pl.when(t == z)
    def _():
        local(kvw_src(g), kvw.at[kvw_slot], "kvw", kvw_slot).start()

    @pl.when(t != z)
    def _():
        kvw_copy(g).start()

    def kvw_received(k, _):
        local(kvw.at[k], kvw.at[k], "kvw", k).wait()
        return 0

    def kvw_sent(k, _):
        kvw_copy(lax.rem(g + k, 8)).wait_send()
        return 0

    def kvw_finish():
        lax.fori_loop(1, 8, kvw_sent, 0)

        @pl.when(t != z)
        def _():
            kvw_copy(g).wait_send()

    pending["kvw"] = lambda: lax.fori_loop(0, 8, kvw_received, 0)
    finish.append(kvw_finish)
    io_all = jnp.concatenate([iog[j].astype(F32) for j in range(8)], axis=0)
    in_vec = io_all[:, :256]
    out_vec = io_all[:, 256:]
    wide = jnp.dot(out_vec.astype(BF16), spread, preferred_element_type=F32)
    row_prompt = lax.rem(lax.div(lax.broadcasted_iota(jnp.int32, (192, 1024), 0), 16), 3)
    col_prompt = lax.div(
        lax.rem(lax.broadcasted_iota(jnp.int32, (192, 1024), 1), 16), 4
    )
    wide = jnp.where(row_prompt == col_prompt, wide, 0.0).astype(BF16)
    arrive("st2")
    start = jnp.dot(wide, st2[...].reshape(1024, 256), preferred_element_type=F32)

    mixed = []
    running = None
    carried = []
    for step in range(4):
        rows = slice(48 * step, 48 * step + 48)
        fall = decay[rows]
        running = fall if running is None else running * fall
        carried = [term * fall for term in carried] + [entering[rows]]
        value = running * start[rows]
        for earlier in range(step + 1):
            match = jnp.sum(
                out_vec[rows] * in_vec[48 * earlier : 48 * earlier + 48], axis=1, keepdims=True
            )
            value = value + match * carried[earlier]
        mixed.append(value + skip * acci[rows, :])
    gate = accg[...]
    gated = jnp.concatenate(mixed, axis=0) * (gate / (1.0 + jnp.exp(-gate)))
    gm[:, own_rows] = (gated * mix_gain[...]).astype(BF16)
    swap("gm", gm.at[:, own_rows], gm.at[:, own_rows], sibling)
    sq[i] = row_sums(gated)
    exchange("sq", 8, i, dev_big_x, lambda j: sq.at[i], lambda j: sq.at[j])
    arrive("sq")
    group_sum = sq[0]
    for j in range(1, 8):
        group_sum = group_sum + sq[j]
    inverse = to_column(lax.rsqrt(group_sum * (1.0 / 2048.0) + 1e-05))
    arrive(("gm", 0), ("loc", 1), ("w", 0))

    my_rows = pl.ds(al(48 * y, 48), 48)
    low = pl.ds(0, 256)
    high = pl.ds(256, 256)

    def rows_of(j):
        return pl.ds(al(48 * j, 48), 48)

    def reduce_scatter(names, left, weight, column, p, a1, b1, sa, sb, a2, b2, zs, zr, use):
        na1, nb1, na2, nb2, nz = names
        tails = ("", "x")

        for c in range(2):

            def block(n, _, c=c):
                xx = lax.div(n, 2)
                hh = lax.rem(n, 2)
                cols = pl.ds(al(1024 * xx + 512 * hh + 256 * c, 256), 256)
                value = jnp.dot(left[...], weight[:, cols], preferred_element_type=F32)
                if column is not None:
                    value = value * column
                p[c, xx, :, pl.ds(al(256 * hh, 256), 256)] = value.astype(BF16)
                return 0

            lax.fori_loop(0, 8, block, 0)
            exchange(
                na1 + tails[c],
                4,
                y,
                dev_y,
                lambda j, c=c: p.at[c, :, rows_of(j), low],
                lambda j, c=c: a1.at[c, j],
            )
            exchange(
                nb1 + tails[c],
                4,
                x,
                dev_x,
                lambda j, c=c: p.at[c, j, :, high],
                lambda j, c=c: b1.at[c, j],
            )
        for c in range(2):
            arrive(na1 + tails[c])
            for xx in range(4):
                total = p[c, xx, my_rows, 0:256].astype(F32)
                for k in range(1, 4):
                    total = total + a1[c, lax.rem(y + k, 4), xx].astype(F32)
                sa[c, xx] = total.astype(BF16)
            exchange(
                na2 + tails[c],
                4,
                x,
                dev_x,
                lambda j, c=c: sa.at[c, j],
                lambda j, c=c: a2.at[c, j],
            )
            arrive(nb1 + tails[c])
            total = p[c, x, :, 256:512].astype(F32)
            for k in range(1, 4):
                total = total + b1[c, lax.rem(x + k, 4)].astype(F32)
            sb[c] = total.astype(BF16)
            exchange(
                nb2 + tails[c],
                4,
                y,
                dev_y,
                lambda j, c=c: sb.at[c, rows_of(j)],
                lambda j, c=c: b2.at[c, j],
            )
        for c in range(2):
            arrive(na2 + tails[c])
            total = sa[c, x].astype(F32)
            for k in range(1, 4):
                total = total + a2[c, lax.rem(x + k, 4)].astype(F32)
            zs[c, :, 0:256] = total.astype(BF16)
            arrive(nb2 + tails[c])
            total = sb[c, my_rows, :].astype(F32)
            for k in range(1, 4):
                total = total + b2[c, lax.rem(y + k, 4)].astype(F32)
            zs[c, :, 256:512] = total.astype(BF16)
            swap(nz, zs.at[c], zr.at[c], zpeer, c)
        for c in range(2):
            arrive((nz, c))
            use(c, zs[c].astype(F32) + zr[c].astype(F32))

    feature = al(1024 * (4 * t + x), 1024)
    squares = []

    def use_mix(c, value):
        spans = [al(feature + 256 * c, 256), al(feature + 512 + 256 * c, 256)]
        old = jnp.concatenate([hid[my_rows, pl.ds(span, 256)] for span in spans], axis=1)
        gain = jnp.concatenate([gain2[:, pl.ds(span, 256)] for span in spans], axis=1)
        residual = old.astype(F32) + value
        res[c] = residual
        mid[c, x, my_rows, :] = (residual * gain).astype(BF16)
        tail = ("", "x")[c]
        exchange(
            "ma1" + tail,
            4,
            x,
            dev_x,
            lambda j: mid.at[c, x, my_rows, low],
            lambda j: mid.at[c, j, my_rows, low],
        )
        exchange(
            "mb1" + tail,
            4,
            y,
            dev_y,
            lambda j: mid.at[c, x, my_rows, high],
            lambda j: mid.at[c, x, rows_of(j), high],
        )
        squares.append(row_sums(residual))

    reduce_scatter(
        ("a1", "b1", "a2", "b2", "rz"),
        gm,
        wm,
        inverse,
        part,
        ra1,
        rb1,
        qa,
        qb,
        ra2,
        rb2,
        rzs,
        rzr,
        use_mix,
    )
    sq2[i] = squares[0] + squares[1]
    exchange("sq2", 8, i, dev_big_x, lambda j: sq2.at[i], lambda j: sq2.at[j])
    for c in range(2):
        tail = ("", "x")[c]
        arrive("ma1" + tail)
        exchange(
            "ma2" + tail,
            4,
            y,
            dev_y,
            lambda j, c=c: mid.at[c, :, my_rows, low],
            lambda j, c=c: mid.at[c, :, rows_of(j), low],
        )
        arrive("mb1" + tail)
        exchange(
            "mb2" + tail,
            4,
            x,
            dev_x,
            lambda j, c=c: mid.at[c, x, :, high],
            lambda j, c=c: mid.at[c, j, :, high],
        )
    arrive("sq2")
    row_sum = sq2[0]
    for j in range(1, 8):
        row_sum = row_sum + sq2[j]
    sqy[y] = row_sum
    exchange("sqy", 4, y, dev_y, lambda j: sqy.at[y], lambda j: sqy.at[j])
    arrive("sqy")
    scale = jnp.concatenate(
        [to_column(lax.rsqrt(sqy[j] * (1.0 / 8192.0) + 1e-05)) for j in range(4)], axis=0
    )

    arrive(("loc", 2), ("w", 1), "kvw")
    query = jnp.zeros((192, 256), F32)
    pair = jnp.zeros((192, 256), F32)
    for c in range(2):
        tail = ("", "x")[c]
        arrive("ma2" + tail, "mb2" + tail)
        for xx in range(4):
            for hh in range(2):
                place = 1024 * xx + 512 * hh + 256 * c
                query = query + jnp.dot(
                    mid[c, xx, :, 256 * hh : 256 * hh + 256],
                    wq[place : place + 256, :],
                    preferred_element_type=F32,
                )
    for xx in range(4):
        pair = pair + jnp.dot(
            mid[lax.rem(x, 2), xx, :, pl.ds(al(256 * lax.div(x, 2), 256), 256)],
            kvw[2 * xx : 2 * xx + 2].reshape(256, 256),
            preferred_element_type=F32,
        )
    pair = pair * scale
    for j in range(8):
        kvp[j] = pair[24 * j : 24 * j + 24]
    exchange("kvr", 8, i, dev_big_x, lambda j: kvp.at[j], lambda j: kvr.at[j])
    qs[...] = query
    swap("q", qs, qr, sibling)

    arrive("kvr")
    pair_sum = kvp[i]
    for k in range(1, 8):
        pair_sum = pair_sum + kvr[lax.rem(i + k, 8)]
    kvg[i] = pair_sum.astype(BF16)
    exchange("kva", 8, i, dev_big_x, lambda j: kvg.at[i], lambda j: kvg.at[j])

    arrive(("q", 0))
    query_rows = ((qs[...] + qr[...]) * (scale * (128.0**-0.5))).astype(BF16)
    arrive("ca2")
    query_of = []
    lane = lax.broadcasted_iota(jnp.int32, (128, 128), 1)
    place = 128 * lax.div(lane, 16) + lax.rem(lane, 16) + 16 * t
    for p in range(3):
        query_p = jnp.concatenate(
            [
                query_rows[48 * step + 16 * p : 48 * step + 16 * p + 16, 128 * head : 128 * head + 128]
                for head in range(2)
                for step in range(4)
            ],
            axis=0,
        )
        query_of.append(query_p)
        for j in range(4):
            keys = ca2[j, p, :, :, 0:128].reshape(128, 128)
            score = nt_dot(query_p, keys)
            scores[p, :, 128 * j : 128 * j + 128] = jnp.where(
                place + 32 * j < lens[p], score, -1e30
            )

    arrive("kva")
    pair_all = jnp.concatenate([kvg[j].astype(F32) for j in range(8)], axis=0)
    row_step = lax.rem(lax.div(lax.broadcasted_iota(jnp.int32, (128, 1), 0), 16), 4)
    row_step = row_step - 4 * t
    wide_lane = lax.broadcasted_iota(jnp.int32, (128, 128), 1)
    for p in range(3):
        far = scores[p]
        top = jnp.max(far, axis=1, keepdims=True)
        near = []
        values = []
        query_p = query_of[p].astype(F32)
        for step in range(4):
            block = pair_all[48 * step + 16 * p : 48 * step + 16 * p + 16]
            tiled = jnp.concatenate([block] * 8, axis=0)
            values.append(tiled[:, 128:])
            score = jnp.sum(query_p * tiled[:, :128], axis=1, keepdims=True)
            score = jnp.where(row_step >= step, score, -1e30)
            near.append(score)
            top = jnp.maximum(top, score)
        far = jnp.exp(far - top)
        near = [jnp.exp(score - top) for score in near]
        total = jnp.sum(far, axis=1, keepdims=True)
        for weight in near:
            total = total + weight
        far = far.astype(BF16)
        result = jnp.zeros((128, 128), F32)
        for j in range(4):
            result = result + jnp.dot(
                far[:, 128 * j : 128 * j + 128],
                ca2[j, p, :, :, 128:256].reshape(128, 128),
                preferred_element_type=F32,
            )
        for weight, value in zip(near, values):
            result = result + weight.astype(BF16).astype(F32) * value
        os[p, :, 0:128] = result
        os[p, :, 128:256] = jnp.where(wide_lane < 64, top, total)
        swap("at", os.at[p], orr.at[p], sibling, p)
    for p in range(3):
        arrive(("at", p))
        mine_top, mine_total = os[p, :, 128:129], os[p, :, 192:193]
        peer_top, peer_total = orr[p, :, 128:129], orr[p, :, 192:193]
        top = jnp.maximum(mine_top, peer_top)
        mine = jnp.exp(mine_top - top)
        peer = jnp.exp(peer_top - top)
        total = mine_total * mine + peer_total * peer
        result = (os[p, :, 0:128] * (mine / total) + orr[p, :, 0:128] * (peer / total)).astype(BF16)
        for head in range(2):
            for step in range(4):
                att[48 * step + 16 * p : 48 * step + 16 * p + 16, 128 * head : 128 * head + 128] = (
                    result[64 * head + 16 * step : 64 * head + 16 * step + 16]
                )

    arrive(("loc", 3), ("w", 2))

    def use_out(c, value):
        value = res[c] + value
        fin[0:48, 256 * c : 256 * c + 256] = value[:, 0:256]
        fin[0:48, 512 + 256 * c : 768 + 256 * c] = value[:, 256:512]

    reduce_scatter(
        ("c1", "d1", "c2", "d2", "sz"),
        att,
        wo,
        None,
        part2,
        rc1,
        rd1,
        qc,
        qd,
        rc2,
        rd2,
        szs,
        szr,
        use_out,
    )

    fin[48:56, :] = jnp.zeros((8, 1024), F32)
    sends = lax.div(y, 2) == z

    def fin_copy(k):
        target = 16 * y + k
        return remote(
            fo.at[k], fi.at[i], "fin", k, i, dev(lax.div(target, 2), lax.rem(target, 2))
        )

    @pl.when(sends)
    def _():
        for k in range(16):
            fo[k] = fin[3 * k : 3 * k + 8, :].astype(BF16)

        def send(k, _):
            @pl.when(16 * y + k == me)
            def _():
                local(fo.at[k], fi.at[i], "fin", i).start()

            @pl.when(16 * y + k != me)
            def _():
                fin_copy(k).start()

            return 0

        lax.fori_loop(0, 16, send, 0)

    def fin_received(k, _):
        local(fi.at[k], fi.at[k], "fin", k).wait()
        return 0

    def fin_finish():
        @pl.when(sends)
        def _():
            def sent(k, _):
                @pl.when(16 * y + k != me)
                def _():
                    fin_copy(k).wait_send()

                return 0

            lax.fori_loop(0, 16, sent, 0)

    lax.fori_loop(0, 8, fin_received, 0)
    finish.append(fin_finish)
    for j in range(8):
        place_j = 1024 * (4 * (j % 2) + j // 2)
        out[:, place_j : place_j + 1024] = fi[j][0:3, :]
    drain()


def scratch():
    def v(shape, dtype=BF16):
        return pltpu.VMEM(shape, dtype)

    reduce_bufs = [
        v((2, 4, 4, 48, 256)),
        v((2, 4, 192, 256)),
        v((2, 4, 48, 256)),
        v((2, 192, 256)),
        v((2, 4, 48, 256)),
        v((2, 4, 48, 256)),
        v((2, 48, 512)),
        v((2, 48, 512)),
    ]
    return [
        v((192, 8192)),
        v((192, 8192)),
        v((8192, 256)),
        v((8192, 256)),
        v((512, 4096)),
        v((4096, 256)),
        v((256, 4096)),
        v((8, 128, 512)),
        v((8, 128, 256)),
        v((8, 8, 16, 256)),
        v((8, 8, 16, 256)),
        v((3, 8, 16, 256)),
        v((4, 3, 8, 16, 256)),
        v((192, 256), F32),
        v((192, 256), F32),
        v((192, 4), F32),
        v((192, 1024)),
        v((8, 24, 512), F32),
        v((8, 24, 512), F32),
        v((8, 24, 512)),
        v((8, 8, 192), F32),
        v((192, 512)),
        v((2, 4, 192, 512)),
        *reduce_bufs,
        v((2, 48, 512), F32),
        v((8, 8, 48), F32),
        v((4, 8, 48), F32),
        v((2, 4, 192, 512)),
        v((192, 256), F32),
        v((192, 256), F32),
        v((8, 24, 256), F32),
        v((8, 24, 256), F32),
        v((8, 24, 256)),
        v((3, 128, 512), F32),
        v((3, 128, 256), F32),
        v((3, 128, 256), F32),
        v((192, 256)),
        v((2, 4, 192, 512)),
        *reduce_bufs,
        v((56, 1024), F32),
        v((16, 8, 1024)),
        v((8, 8, 1024)),
        pltpu.SemaphoreType.DMA((len(STAGES), 16)),
        pltpu.SemaphoreType.DMA((len(STAGES), 16)),
    ]


def shards(
    hidden_input,
    prompt_lengths,
    prompt_states,
    prompt_cache,
    input_gain,
    gate_weight,
    input_weight,
    rate_weight,
    rate_bias,
    decay_log,
    skip_gain,
    state_io_weight,
    mix_gain,
    mix_weight,
    middle_gain,
    query_weight,
    key_value_weight,
    output_weight,
):
    hidden = hidden_input.reshape(192, 8192)
    states = jnp.pad(prompt_states.astype(BF16), ((0, 1), (0, 0), (0, 0), (0, 0)))
    states = states.reshape(4, 8, 8, 4, 64, 4).transpose(2, 1, 0, 5, 3, 4).reshape(8, 8, 16, 256)
    cache = prompt_cache.transpose(2, 0, 1, 3)
    vmem = pl.BlockSpec(memory_space=pltpu.VMEM)
    smem = pl.BlockSpec(memory_space=pltpu.SMEM)
    anyw = pl.BlockSpec(memory_space=pl.ANY)
    return pl.pallas_call(
        kernel,
        out_shape=jax.ShapeDtypeStruct((3, 8192), BF16),
        in_specs=[
            smem,
            anyw,
            anyw,
            anyw,
            vmem,
            anyw,
            anyw,
            vmem,
            vmem,
            vmem,
            vmem,
            vmem,
            anyw,
            anyw,
            vmem,
            anyw,
            anyw,
            anyw,
        ],
        out_specs=vmem,
        scratch_shapes=scratch(),
        compiler_params=pltpu.CompilerParams(
            collective_id=0, has_side_effects=True, vmem_limit_bytes=60 * 1024 * 1024
        ),
        cost_estimate=pl.CostEstimate(
            flops=4_000_000_000, bytes_accessed=24_000_000, transcendentals=1_000_000
        ),
    )(
        prompt_lengths,
        hidden,
        states,
        cache,
        input_gain[None, :],
        gate_weight,
        input_weight,
        rate_weight.T,
        rate_bias[None, :],
        decay_log[None, :],
        skip_gain[None, :],
        mix_gain[None, :],
        state_io_weight,
        mix_weight,
        middle_gain[None, :],
        query_weight,
        key_value_weight,
        output_weight,
    )


def solution(mesh):
    in_specs = (
        P(None, "prompt", None),
        P("prompt"),
        P("prompt", None, None, ("sample", "tensor")),
        P("prompt", ("sample", "tensor"), None, None),
        P(),
        P(None, ("sample", "tensor")),
        P(None, ("sample", "tensor")),
        P(None, ("sample", "tensor")),
        P(("sample", "tensor")),
        P(("sample", "tensor")),
        P(("sample", "tensor")),
        P(("sample", "tensor"), None),
        P(("sample", "tensor")),
        P(("sample", "tensor"), None),
        P(),
        P(None, ("sample", "tensor")),
        P(("sample", "tensor"), None),
        P(("sample", "tensor"), None),
    )
    out_specs = P(("prompt", "sample", "tensor"), None)
    return jax.shard_map(shards, mesh=mesh, in_specs=in_specs, out_specs=out_specs, check_vma=False)
```

```python
import jax
import jax.numpy as jnp
from jax import lax
from jax.experimental import pallas as pl
from jax.experimental.pallas import tpu as pltpu
from jax.sharding import PartitionSpec as P

F32 = jnp.float32
BF16 = jnp.bfloat16
MESH = pl.DeviceIdType.MESH
HIGH = lax.Precision.HIGHEST

STAGES = (
    "wio",
    "st1",
    "kvw",
    "kvx",
    "ca1",
    "st2",
    "ca2",
    "iors",
    "ioag",
    "sq",
    "gm",
    "a1",
    "b1",
    "a2",
    "b2",
    "sq2",
    "sqy",
    "ma1",
    "mb1",
    "ma2",
    "mb2",
    "q",
    "kvr",
    "kva",
    "c1",
    "d1",
    "c2",
    "d2",
    "fin",
    "a1x",
    "b1x",
    "a2x",
    "b2x",
    "ma1x",
    "mb1x",
    "ma2x",
    "mb2x",
    "c1x",
    "d1x",
    "c2x",
    "d2x",
    "w0",
    "w1",
    "w2",
    "loc0",
    "loc1",
    "loc2",
    "loc3",
    "rz0",
    "rz1",
    "sz0",
    "sz1",
    "at0",
    "at1",
    "at2",
    "pro",
)
STAGE = {name: number for number, name in enumerate(STAGES)}


def nt_dot(left, right, precision=None):
    return lax.dot_general(
        left, right, (((1,), (1,)), ((), ())), preferred_element_type=F32, precision=precision
    )


def row_sums(values):
    ones = jnp.ones((8, values.shape[1]), F32)
    return nt_dot(ones, values * values, HIGH)


def to_column(rows):
    size = rows.shape[1]
    eye = (
        lax.broadcasted_iota(jnp.int32, (size, size), 0)
        == lax.broadcasted_iota(jnp.int32, (size, size), 1)
    ).astype(F32)
    return nt_dot(eye, rows, HIGH)[:, :1]


def kernel(
    lens,
    hid_h,
    st_h,
    cache_h,
    gain1,
    wg_h,
    wi_h,
    wrt,
    rate_bias,
    decay_log,
    skip_gain,
    mix_gain,
    wio_h,
    wm_h,
    gain2,
    wq_h,
    wkv_h,
    wo_h,
    out,
    hid,
    nrm,
    wg,
    wi,
    wm,
    wq,
    wo,
    wio,
    kvw,
    st1,
    st2,
    ca1,
    ca2,
    accg,
    acci,
    accr,
    nio,
    iop,
    ior,
    iog,
    sq,
    gm,
    part,
    ra1,
    rb1,
    qa,
    qb,
    ra2,
    rb2,
    rzs,
    rzr,
    res,
    sq2,
    sqy,
    mid,
    qs,
    qr,
    kvp,
    kvr,
    kvg,
    scores,
    os,
    orr,
    att,
    part2,
    rc1,
    rd1,
    qc,
    qd,
    rc2,
    rd2,
    szs,
    szr,
    fin,
    fo,
    fi,
    ssem,
    rsem,
    psem,
):
    s = lax.axis_index("sample")
    t = lax.axis_index("tensor")
    z = lax.div(s, 16)
    y = lax.rem(lax.div(s, 4), 4)
    x = lax.rem(s, 4)
    g = lax.div(s, 4)
    i = 2 * x + t

    def al(value, size):
        return pl.multiple_of(value, size)

    def dev(sample, tensor):
        return {"sample": sample, "tensor": tensor}

    def dev_big_x(j):
        return dev(4 * g + lax.div(j, 2), lax.rem(j, 2))

    def dev_big_y(j):
        return dev(4 * j + x, t)

    def dev_x(j):
        return dev(4 * g + j, t)

    def dev_y(j):
        return dev(16 * z + 4 * j + x, t)

    sibling = dev(s, 1 - t)
    zpeer = dev(16 * (1 - z) + 4 * y + x, t)

    def remote(src, dst, stage, device, landing=None):
        return pltpu.make_async_remote_copy(
            src_ref=src,
            dst_ref=dst,
            send_sem=ssem.at[STAGE[stage]],
            recv_sem=rsem.at[STAGE[landing or stage]],
            device_id=device,
            device_id_type=MESH,
        )

    def local(src, dst, stage):
        return pltpu.make_async_copy(src, dst, rsem.at[STAGE[stage]])

    def all_sent(ref, stage):
        pltpu.make_async_copy(ref, ref, ssem.at[STAGE[stage]]).wait()

    pending = {}
    finish = []

    def exchange(stage, size, me, device, src_of, dst_of, span, own=False):
        def send(k, _):
            j = lax.rem(me + k, size)
            remote(src_of(j), dst_of(me), stage, device(j)).start()
            return 0

        if own:
            local(src_of(me), dst_of(me), stage).start()
        lax.fori_loop(1, size, send, 0)
        landed = span(size if own else size - 1)
        left = span(size - 1)
        pending[stage] = local(landed, landed, stage).wait
        finish.append(lambda: all_sent(left, stage))

    def swap(stage, src, dst, device):
        copy = remote(src, dst, stage, device)
        copy.start()
        pending[stage] = copy.wait_recv
        finish.append(copy.wait_send)

    def fetch(stage, src, dst):
        copy = local(src, dst, stage)
        copy.start()
        pending[stage] = copy.wait

    def arrive(*names):
        for name in names:
            pending.pop(name)()

    def drain():
        for name in list(pending):
            arrive(name)
        for wait in finish:
            wait()

    fetch("loc0", hid_h, hid)

    def proj_copy(c, src, dst, slot):
        rows = pl.ds(al(c * 2048, 2048), 2048)
        return pltpu.make_async_copy(src.at[rows], dst.at[rows], psem.at[2 * c + slot])

    def start_proj(c, _):
        proj_copy(c, wg_h, wg, 0).start()
        proj_copy(c, wi_h, wi, 1).start()
        return 0

    lax.fori_loop(0, 4, start_proj, 0)

    def project_wait(c, _):
        proj_copy(c, wg_h, wg, 0).wait()
        proj_copy(c, wi_h, wi, 1).wait()
        return 0

    pending["pro"] = lambda: lax.fori_loop(0, 4, project_wait, 0)

    barrier = pltpu.get_barrier_semaphore()
    me = 2 * s + t

    def greet(k, _):
        j = lax.rem(me + k, 64)
        pl.semaphore_signal(
            barrier, inc=1, device_id=dev(lax.div(j, 2), lax.rem(j, 2)), device_id_type=MESH
        )
        return 0

    lax.fori_loop(1, 64, greet, 0)
    pl.semaphore_wait(barrier, 63)

    def wio_src(j):
        return wio_h.at[:, pl.ds(al(512 * j, 512), 512)]

    exchange("ca1", 8, g, dev_big_y, lambda j: cache_h.at[j], lambda j: ca1.at[:, j], lambda n: ca1.at[:, pl.ds(0, n)], own=True)
    exchange("st1", 8, i, dev_big_x, lambda j: st_h.at[j], lambda j: st1.at[j], lambda n: st1.at[pl.ds(0, n)], own=True)
    exchange("wio", 8, g, dev_big_y, wio_src, lambda j: wio.at[j], lambda n: wio.at[pl.ds(0, n)], own=True)

    half = al(4096 * t, 4096)
    other = al(4096 * (1 - t), 4096)
    own_rows = pl.ds(al(256 * t, 256), 256)
    head_rows = pl.ds(al(128 * t, 128), 128)
    fetch("loc1", wm_h.at[:, pl.ds(half, 4096)], wm.at[own_rows])
    swap("w0", wm_h.at[:, pl.ds(other, 4096)], wm.at[own_rows], sibling)
    fetch("loc2", wq_h.at[pl.ds(half, 4096)], wq.at[:, head_rows])
    swap("w1", wq_h.at[pl.ds(other, 4096)], wq.at[:, head_rows], sibling)
    fetch("loc3", wo_h.at[:, pl.ds(half, 4096)], wo.at[head_rows])
    swap("w2", wo_h.at[:, pl.ds(other, 4096)], wo.at[head_rows], sibling)

    arrive("loc0")

    def norm_rows(r, _):
        rows = pl.ds(al(16 * r, 16), 16)
        values = hid[rows, :].astype(F32)
        scale = lax.rsqrt(jnp.mean(values * values, axis=1, keepdims=True) + 1e-05)
        nrm[rows, :] = (values * scale * gain1[...]).astype(BF16)
        return 0

    lax.fori_loop(0, 12, norm_rows, 0)
    arrive("ca1")
    exchange("ca2", 4, x, dev_x, lambda j: ca1, lambda j: ca2.at[j], lambda n: ca2.at[pl.ds(0, n)], own=True)

    accg[...] = jnp.zeros_like(accg)
    acci[...] = jnp.zeros_like(acci)
    accr[...] = jnp.zeros_like(accr)

    pending.pop("pro")

    def project(c, _):
        project_wait(c, 0)
        span = pl.ds(al(c * 2048, 2048), 2048)
        left = nrm[:, span]
        accg[...] += jnp.dot(left, wg[span, :], preferred_element_type=F32)
        acci[...] += jnp.dot(left, wi[span, :], preferred_element_type=F32)
        accr[...] += nt_dot(left, wrt[:, span])
        return 0

    lax.fori_loop(0, 4, project, 0)

    def pick(c, _):
        nio[:, pl.ds(al(128 * c, 128), 128)] = nrm[:, pl.ds(al(128 * (8 * c + i), 128), 128)]
        return 0

    lax.fori_loop(0, 8, pick, 0)
    arrive("wio", "st1")
    exchange("st2", 8, g, dev_big_y, lambda j: st1.at[:, j], lambda j: st2.at[j], lambda n: st2.at[pl.ds(0, n)], own=True)
    io_part = jnp.dot(nio[...], wio[...].reshape(1024, 512), preferred_element_type=F32)
    for j in range(8):
        iop[j] = io_part[24 * j : 24 * j + 24]
    exchange("iors", 8, i, dev_big_x, lambda j: iop.at[j], lambda j: ior.at[j], lambda n: ior.at[pl.ds(0, n)])
    arrive("iors")
    io_sum = iop[i]
    for k in range(1, 8):
        io_sum = io_sum + ior[lax.rem(i + k, 8)]
    iog[i] = io_sum.astype(BF16)
    exchange("ioag", 8, i, dev_big_x, lambda j: iog.at[i], lambda j: iog.at[j], lambda n: iog.at[pl.ds(0, n)])

    lift = (
        lax.broadcasted_iota(jnp.int32, (4, 256), 0)
        == lax.div(lax.broadcasted_iota(jnp.int32, (4, 256), 1), 64)
    ).astype(F32)

    def widen(heads):
        return jnp.dot(heads, lift, preferred_element_type=F32, precision=HIGH)

    raw = widen(accr[...] + rate_bias[...])
    rate = jnp.maximum(raw, 0.0) + jnp.log1p(jnp.exp(-jnp.abs(raw)))
    decay = jnp.exp(rate * -jnp.exp(widen(decay_log[...])))
    skip = widen(skip_gain[...])
    entering = rate * acci[...]
    column = lax.broadcasted_iota(jnp.int32, (256, 1024), 1)
    inside = lax.rem(column, 16)
    owner = lax.div(column, 16)
    spread = (
        (4 * owner + lax.rem(inside, 4) == lax.broadcasted_iota(jnp.int32, (256, 1024), 0))
        & (inside < 12)
    )
    spread = jnp.where(spread, 1.0, 0.0).astype(BF16)

    arrive("ioag")
    def kvw_src(j):
        return wkv_h.at[:, pl.ds(al(256 * j, 256), 256)]

    kvw_slot = 2 * y + t

    def kvw_copy(j, stage):
        return remote(kvw_src(j), kvw.at[kvw_slot], stage, dev(4 * j + x, z), "kvw")

    def kvw_send(k, _):
        kvw_copy(lax.rem(g + k, 8), "kvw").start()
        return 0

    lax.fori_loop(1, 8, kvw_send, 0)

    @pl.when(t == z)
    def _():
        local(kvw_src(g), kvw.at[kvw_slot], "kvw").start()

    @pl.when(t != z)
    def _():
        kvw_copy(g, "kvx").start()

    def kvw_finish():
        all_sent(kvw.at[pl.ds(0, 7)], "kvw")

        @pl.when(t != z)
        def _():
            kvw_copy(g, "kvx").wait_send()

    pending["kvw"] = local(kvw, kvw, "kvw").wait
    finish.append(kvw_finish)
    io_all = jnp.concatenate([iog[j].astype(F32) for j in range(8)], axis=0)
    in_vec = io_all[:, :256]
    out_vec = io_all[:, 256:]
    wide = jnp.dot(out_vec.astype(BF16), spread, preferred_element_type=F32)
    row_prompt = lax.rem(lax.div(lax.broadcasted_iota(jnp.int32, (192, 1024), 0), 16), 3)
    col_prompt = lax.div(
        lax.rem(lax.broadcasted_iota(jnp.int32, (192, 1024), 1), 16), 4
    )
    wide = jnp.where(row_prompt == col_prompt, wide, 0.0).astype(BF16)
    arrive("st2")
    start = jnp.dot(wide, st2[...].reshape(1024, 256), preferred_element_type=F32)

    mixed = []
    running = None
    carried = []
    for step in range(4):
        rows = slice(48 * step, 48 * step + 48)
        fall = decay[rows]
        running = fall if running is None else running * fall
        carried = [term * fall for term in carried] + [entering[rows]]
        value = running * start[rows]
        for earlier in range(step + 1):
            match = jnp.sum(
                out_vec[rows] * in_vec[48 * earlier : 48 * earlier + 48], axis=1, keepdims=True
            )
            value = value + match * carried[earlier]
        mixed.append(value + skip * acci[rows, :])
    gate = accg[...]
    gated = jnp.concatenate(mixed, axis=0) * (gate / (1.0 + jnp.exp(-gate)))
    gm[:, own_rows] = (gated * mix_gain[...]).astype(BF16)
    swap("gm", gm.at[:, own_rows], gm.at[:, own_rows], sibling)
    sq[i] = row_sums(gated)
    exchange("sq", 8, i, dev_big_x, lambda j: sq.at[i], lambda j: sq.at[j], lambda n: sq.at[pl.ds(0, n)])
    arrive("sq")
    group_sum = sq[0]
    for j in range(1, 8):
        group_sum = group_sum + sq[j]
    inverse = to_column(lax.rsqrt(group_sum * (1.0 / 2048.0) + 1e-05))
    arrive("gm", "loc1", "w0")

    my_rows = pl.ds(al(48 * y, 48), 48)
    low = pl.ds(0, 256)
    high = pl.ds(256, 256)

    def rows_of(j):
        return pl.ds(al(48 * j, 48), 48)

    def reduce_scatter(names, left, weight, column, p, a1, b1, sa, sb, a2, b2, zs, zr, use):
        na1, nb1, na2, nb2, nz = names
        tails = ("", "x")

        for c in range(2):

            def block(n, _, c=c):
                xx = lax.div(n, 2)
                hh = lax.rem(n, 2)
                cols = pl.ds(al(1024 * xx + 512 * hh + 256 * c, 256), 256)
                value = jnp.dot(left[...], weight[:, cols], preferred_element_type=F32)
                if column is not None:
                    value = value * column
                p[c, xx, :, pl.ds(al(256 * hh, 256), 256)] = value.astype(BF16)
                return 0

            lax.fori_loop(0, 8, block, 0)
            exchange(
                na1 + tails[c],
                4,
                y,
                dev_y,
                lambda j, c=c: p.at[c, :, rows_of(j), low],
                lambda j, c=c: a1.at[c, j],
                lambda n, c=c: a1.at[c, pl.ds(0, n)],
            )
            exchange(
                nb1 + tails[c],
                4,
                x,
                dev_x,
                lambda j, c=c: p.at[c, j, :, high],
                lambda j, c=c: b1.at[c, j],
                lambda n, c=c: b1.at[c, pl.ds(0, n)],
            )
        for c in range(2):
            arrive(na1 + tails[c])
            for xx in range(4):
                total = p[c, xx, my_rows, 0:256].astype(F32)
                for k in range(1, 4):
                    total = total + a1[c, lax.rem(y + k, 4), xx].astype(F32)
                sa[c, xx] = total.astype(BF16)
            exchange(
                na2 + tails[c],
                4,
                x,
                dev_x,
                lambda j, c=c: sa.at[c, j],
                lambda j, c=c: a2.at[c, j],
                lambda n, c=c: a2.at[c, pl.ds(0, n)],
            )
            arrive(nb1 + tails[c])
            total = p[c, x, :, 256:512].astype(F32)
            for k in range(1, 4):
                total = total + b1[c, lax.rem(x + k, 4)].astype(F32)
            sb[c] = total.astype(BF16)
            exchange(
                nb2 + tails[c],
                4,
                y,
                dev_y,
                lambda j, c=c: sb.at[c, rows_of(j)],
                lambda j, c=c: b2.at[c, j],
                lambda n, c=c: b2.at[c, pl.ds(0, n)],
            )
        for c in range(2):
            arrive(na2 + tails[c])
            total = sa[c, x].astype(F32)
            for k in range(1, 4):
                total = total + a2[c, lax.rem(x + k, 4)].astype(F32)
            zs[c, :, 0:256] = total.astype(BF16)
            arrive(nb2 + tails[c])
            total = sb[c, my_rows, :].astype(F32)
            for k in range(1, 4):
                total = total + b2[c, lax.rem(y + k, 4)].astype(F32)
            zs[c, :, 256:512] = total.astype(BF16)
            swap(nz + str(c), zs.at[c], zr.at[c], zpeer)
        for c in range(2):
            arrive(nz + str(c))
            use(c, zs[c].astype(F32) + zr[c].astype(F32))

    feature = al(1024 * (4 * t + x), 1024)
    squares = []

    def use_mix(c, value):
        spans = [al(feature + 256 * c, 256), al(feature + 512 + 256 * c, 256)]
        old = jnp.concatenate([hid[my_rows, pl.ds(span, 256)] for span in spans], axis=1)
        gain = jnp.concatenate([gain2[:, pl.ds(span, 256)] for span in spans], axis=1)
        residual = old.astype(F32) + value
        res[c] = residual
        mid[c, x, my_rows, :] = (residual * gain).astype(BF16)
        tail = ("", "x")[c]
        exchange(
            "ma1" + tail,
            4,
            x,
            dev_x,
            lambda j: mid.at[c, x, my_rows, low],
            lambda j: mid.at[c, j, my_rows, low],
            lambda n: mid.at[c, pl.ds(0, n), my_rows, low],
        )
        exchange(
            "mb1" + tail,
            4,
            y,
            dev_y,
            lambda j: mid.at[c, x, my_rows, high],
            lambda j: mid.at[c, x, rows_of(j), high],
            lambda n: mid.at[c, x, pl.ds(0, 48 * n), high],
        )
        squares.append(row_sums(residual))

    reduce_scatter(
        ("a1", "b1", "a2", "b2", "rz"),
        gm,
        wm,
        inverse,
        part,
        ra1,
        rb1,
        qa,
        qb,
        ra2,
        rb2,
        rzs,
        rzr,
        use_mix,
    )
    sq2[i] = squares[0] + squares[1]
    exchange("sq2", 8, i, dev_big_x, lambda j: sq2.at[i], lambda j: sq2.at[j], lambda n: sq2.at[pl.ds(0, n)])
    for c in range(2):
        tail = ("", "x")[c]
        arrive("ma1" + tail)
        exchange(
            "ma2" + tail,
            4,
            y,
            dev_y,
            lambda j, c=c: mid.at[c, :, my_rows, low],
            lambda j, c=c: mid.at[c, :, rows_of(j), low],
            lambda n, c=c: mid.at[c, :, pl.ds(0, 48 * n), low],
        )
        arrive("mb1" + tail)
        exchange(
            "mb2" + tail,
            4,
            x,
            dev_x,
            lambda j, c=c: mid.at[c, x, :, high],
            lambda j, c=c: mid.at[c, j, :, high],
            lambda n, c=c: mid.at[c, pl.ds(0, n), :, high],
        )
    arrive("sq2")
    row_sum = sq2[0]
    for j in range(1, 8):
        row_sum = row_sum + sq2[j]
    sqy[y] = row_sum
    exchange("sqy", 4, y, dev_y, lambda j: sqy.at[y], lambda j: sqy.at[j], lambda n: sqy.at[pl.ds(0, n)])
    arrive("sqy")
    scale = jnp.concatenate(
        [to_column(lax.rsqrt(sqy[j] * (1.0 / 8192.0) + 1e-05)) for j in range(4)], axis=0
    )

    arrive("loc2", "w1", "kvw")
    query = jnp.zeros((192, 256), F32)
    pair = jnp.zeros((192, 256), F32)
    for c in range(2):
        tail = ("", "x")[c]
        arrive("ma2" + tail, "mb2" + tail)
        for xx in range(4):
            for hh in range(2):
                place = 1024 * xx + 512 * hh + 256 * c
                query = query + jnp.dot(
                    mid[c, xx, :, 256 * hh : 256 * hh + 256],
                    wq[place : place + 256, :],
                    preferred_element_type=F32,
                )
    for xx in range(4):
        pair = pair + jnp.dot(
            mid[lax.rem(x, 2), xx, :, pl.ds(al(256 * lax.div(x, 2), 256), 256)],
            kvw[2 * xx : 2 * xx + 2].reshape(256, 256),
            preferred_element_type=F32,
        )
    pair = pair * scale
    for j in range(8):
        kvp[j] = pair[24 * j : 24 * j + 24]
    exchange("kvr", 8, i, dev_big_x, lambda j: kvp.at[j], lambda j: kvr.at[j], lambda n: kvr.at[pl.ds(0, n)])
    qs[...] = query
    swap("q", qs, qr, sibling)

    arrive("kvr")
    pair_sum = kvp[i]
    for k in range(1, 8):
        pair_sum = pair_sum + kvr[lax.rem(i + k, 8)]
    kvg[i] = pair_sum.astype(BF16)
    exchange("kva", 8, i, dev_big_x, lambda j: kvg.at[i], lambda j: kvg.at[j], lambda n: kvg.at[pl.ds(0, n)])

    arrive("q")
    query_rows = ((qs[...] + qr[...]) * (scale * (128.0**-0.5))).astype(BF16)
    arrive("ca2")
    query_of = []
    lane = lax.broadcasted_iota(jnp.int32, (128, 128), 1)
    place = 128 * lax.div(lane, 16) + lax.rem(lane, 16) + 16 * t
    for p in range(3):
        query_p = jnp.concatenate(
            [
                query_rows[48 * step + 16 * p : 48 * step + 16 * p + 16, 128 * head : 128 * head + 128]
                for head in range(2)
                for step in range(4)
            ],
            axis=0,
        )
        query_of.append(query_p)
        for j in range(4):
            keys = ca2[j, p, :, :, 0:128].reshape(128, 128)
            score = nt_dot(query_p, keys)
            scores[p, :, 128 * j : 128 * j + 128] = jnp.where(
                place + 32 * j < lens[p], score, -1e30
            )

    arrive("kva")
    pair_all = jnp.concatenate([kvg[j].astype(F32) for j in range(8)], axis=0)
    row_step = lax.rem(lax.div(lax.broadcasted_iota(jnp.int32, (128, 1), 0), 16), 4)
    row_step = row_step - 4 * t
    wide_lane = lax.broadcasted_iota(jnp.int32, (128, 128), 1)
    for p in range(3):
        far = scores[p]
        top = jnp.max(far, axis=1, keepdims=True)
        near = []
        values = []
        query_p = query_of[p].astype(F32)
        for step in range(4):
            block = pair_all[48 * step + 16 * p : 48 * step + 16 * p + 16]
            tiled = jnp.concatenate([block] * 8, axis=0)
            values.append(tiled[:, 128:])
            score = jnp.sum(query_p * tiled[:, :128], axis=1, keepdims=True)
            score = jnp.where(row_step >= step, score, -1e30)
            near.append(score)
            top = jnp.maximum(top, score)
        far = jnp.exp(far - top)
        near = [jnp.exp(score - top) for score in near]
        total = jnp.sum(far, axis=1, keepdims=True)
        for weight in near:
            total = total + weight
        far = far.astype(BF16)
        result = jnp.zeros((128, 128), F32)
        for j in range(4):
            result = result + jnp.dot(
                far[:, 128 * j : 128 * j + 128],
                ca2[j, p, :, :, 128:256].reshape(128, 128),
                preferred_element_type=F32,
            )
        for weight, value in zip(near, values):
            result = result + weight.astype(BF16).astype(F32) * value
        os[p, :, 0:128] = result
        os[p, :, 128:256] = jnp.where(wide_lane < 64, top, total)
        swap("at" + str(p), os.at[p], orr.at[p], sibling)
    for p in range(3):
        arrive("at" + str(p))
        mine_top, mine_total = os[p, :, 128:129], os[p, :, 192:193]
        peer_top, peer_total = orr[p, :, 128:129], orr[p, :, 192:193]
        top = jnp.maximum(mine_top, peer_top)
        mine = jnp.exp(mine_top - top)
        peer = jnp.exp(peer_top - top)
        total = mine_total * mine + peer_total * peer
        result = (os[p, :, 0:128] * (mine / total) + orr[p, :, 0:128] * (peer / total)).astype(BF16)
        for head in range(2):
            for step in range(4):
                att[48 * step + 16 * p : 48 * step + 16 * p + 16, 128 * head : 128 * head + 128] = (
                    result[64 * head + 16 * step : 64 * head + 16 * step + 16]
                )

    arrive("loc3", "w2")

    def use_out(c, value):
        value = res[c] + value
        fin[0:48, 256 * c : 256 * c + 256] = value[:, 0:256]
        fin[0:48, 512 + 256 * c : 768 + 256 * c] = value[:, 256:512]

    reduce_scatter(
        ("c1", "d1", "c2", "d2", "sz"),
        att,
        wo,
        None,
        part2,
        rc1,
        rd1,
        qc,
        qd,
        rc2,
        rd2,
        szs,
        szr,
        use_out,
    )

    fin[48:56, :] = jnp.zeros((8, 1024), F32)
    sends = lax.div(y, 2) == z

    def fin_copy(k):
        target = 16 * y + k
        return remote(fo.at[k], fi.at[i], "fin", dev(lax.div(target, 2), lax.rem(target, 2)))

    @pl.when(sends)
    def _():
        for k in range(16):
            fo[k] = fin[3 * k : 3 * k + 8, :].astype(BF16)

        def send(k, _):
            @pl.when(16 * y + k == me)
            def _():
                local(fo.at[k], fi.at[i], "fin").start()

            @pl.when(16 * y + k != me)
            def _():
                fin_copy(k).start()

            return 0

        lax.fori_loop(0, 16, send, 0)

    keeps = sends & (lax.div(me, 16) == y)

    def fin_finish():
        @pl.when(keeps)
        def _():
            all_sent(fo.at[pl.ds(0, 15)], "fin")

        @pl.when(sends & (lax.div(me, 16) != y))
        def _():
            all_sent(fo, "fin")

    local(fi, fi, "fin").wait()
    finish.append(fin_finish)
    for j in range(8):
        place_j = 1024 * (4 * (j % 2) + j // 2)
        out[:, place_j : place_j + 1024] = fi[j][0:3, :]
    drain()


def scratch():
    def v(shape, dtype=BF16):
        return pltpu.VMEM(shape, dtype)

    reduce_bufs = [
        v((2, 4, 4, 48, 256)),
        v((2, 4, 192, 256)),
        v((2, 4, 48, 256)),
        v((2, 192, 256)),
        v((2, 4, 48, 256)),
        v((2, 4, 48, 256)),
        v((2, 48, 512)),
        v((2, 48, 512)),
    ]
    return [
        v((192, 8192)),
        v((192, 8192)),
        v((8192, 256)),
        v((8192, 256)),
        v((512, 4096)),
        v((4096, 256)),
        v((256, 4096)),
        v((8, 128, 512)),
        v((8, 128, 256)),
        v((8, 8, 16, 256)),
        v((8, 8, 16, 256)),
        v((3, 8, 16, 256)),
        v((4, 3, 8, 16, 256)),
        v((192, 256), F32),
        v((192, 256), F32),
        v((192, 4), F32),
        v((192, 1024)),
        v((8, 24, 512), F32),
        v((8, 24, 512), F32),
        v((8, 24, 512)),
        v((8, 8, 192), F32),
        v((192, 512)),
        v((2, 4, 192, 512)),
        *reduce_bufs,
        v((2, 48, 512), F32),
        v((8, 8, 48), F32),
        v((4, 8, 48), F32),
        v((2, 4, 192, 512)),
        v((192, 256), F32),
        v((192, 256), F32),
        v((8, 24, 256), F32),
        v((8, 24, 256), F32),
        v((8, 24, 256)),
        v((3, 128, 512), F32),
        v((3, 128, 256), F32),
        v((3, 128, 256), F32),
        v((192, 256)),
        v((2, 4, 192, 512)),
        *reduce_bufs,
        v((56, 1024), F32),
        v((16, 8, 1024)),
        v((8, 8, 1024)),
        pltpu.SemaphoreType.DMA((len(STAGES),)),
        pltpu.SemaphoreType.DMA((len(STAGES),)),
        pltpu.SemaphoreType.DMA((8,)),
    ]


def shards(
    hidden_input,
    prompt_lengths,
    prompt_states,
    prompt_cache,
    input_gain,
    gate_weight,
    input_weight,
    rate_weight,
    rate_bias,
    decay_log,
    skip_gain,
    state_io_weight,
    mix_gain,
    mix_weight,
    middle_gain,
    query_weight,
    key_value_weight,
    output_weight,
):
    hidden = hidden_input.reshape(192, 8192)
    states = jnp.pad(prompt_states.astype(BF16), ((0, 1), (0, 0), (0, 0), (0, 0)))
    states = states.reshape(4, 8, 8, 4, 64, 4).transpose(2, 1, 0, 5, 3, 4).reshape(8, 8, 16, 256)
    cache = prompt_cache.transpose(2, 0, 1, 3)
    vmem = pl.BlockSpec(memory_space=pltpu.VMEM)
    smem = pl.BlockSpec(memory_space=pltpu.SMEM)
    anyw = pl.BlockSpec(memory_space=pl.ANY)
    return pl.pallas_call(
        kernel,
        out_shape=jax.ShapeDtypeStruct((3, 8192), BF16),
        in_specs=[
            smem,
            anyw,
            anyw,
            anyw,
            vmem,
            anyw,
            anyw,
            vmem,
            vmem,
            vmem,
            vmem,
            vmem,
            anyw,
            anyw,
            vmem,
            anyw,
            anyw,
            anyw,
        ],
        out_specs=vmem,
        scratch_shapes=scratch(),
        compiler_params=pltpu.CompilerParams(
            collective_id=0, has_side_effects=True, vmem_limit_bytes=60 * 1024 * 1024
        ),
        cost_estimate=pl.CostEstimate(
            flops=4_000_000_000, bytes_accessed=24_000_000, transcendentals=1_000_000
        ),
    )(
        prompt_lengths,
        hidden,
        states,
        cache,
        input_gain[None, :],
        gate_weight,
        input_weight,
        rate_weight.T,
        rate_bias[None, :],
        decay_log[None, :],
        skip_gain[None, :],
        mix_gain[None, :],
        state_io_weight,
        mix_weight,
        middle_gain[None, :],
        query_weight,
        key_value_weight,
        output_weight,
    )


def solution(mesh):
    in_specs = (
        P(None, "prompt", None),
        P("prompt"),
        P("prompt", None, None, ("sample", "tensor")),
        P("prompt", ("sample", "tensor"), None, None),
        P(),
        P(None, ("sample", "tensor")),
        P(None, ("sample", "tensor")),
        P(None, ("sample", "tensor")),
        P(("sample", "tensor")),
        P(("sample", "tensor")),
        P(("sample", "tensor")),
        P(("sample", "tensor"), None),
        P(("sample", "tensor")),
        P(("sample", "tensor"), None),
        P(),
        P(None, ("sample", "tensor")),
        P(("sample", "tensor"), None),
        P(("sample", "tensor"), None),
    )
    out_specs = P(("prompt", "sample", "tensor"), None)
    return jax.shard_map(shards, mesh=mesh, in_specs=in_specs, out_specs=out_specs, check_vma=False)
```

```python
import jax
import jax.numpy as jnp
from jax import lax
from jax.experimental import pallas as pl
from jax.experimental.pallas import tpu as pltpu
from jax.sharding import PartitionSpec as P

F32 = jnp.float32
BF16 = jnp.bfloat16
MESH = pl.DeviceIdType.MESH
HIGH = lax.Precision.HIGHEST

STAGES = (
    "wio",
    "st1",
    "kvw",
    "kvx",
    "ca1",
    "st2",
    "ca2",
    "iors",
    "ioag",
    "sq",
    "gm",
    "a1",
    "b1",
    "a2",
    "b2",
    "sq2",
    "sqy",
    "ma1",
    "mb1",
    "ma2",
    "mb2",
    "q",
    "kvr",
    "kva",
    "c1",
    "d1",
    "c2",
    "d2",
    "fin",
    "a1x",
    "b1x",
    "a2x",
    "b2x",
    "ma1x",
    "mb1x",
    "ma2x",
    "mb2x",
    "c1x",
    "d1x",
    "c2x",
    "d2x",
    "w0",
    "w1",
    "w2",
    "loc0",
    "loc1",
    "loc2",
    "loc3",
    "loc4",
    "a1r",
    "a1d",
    "a1c",
    "a1xr",
    "a1xd",
    "a1xc",
    "b1r",
    "b1d",
    "b1c",
    "b1xr",
    "b1xd",
    "b1xc",
    "c1r",
    "c1d",
    "c1c",
    "c1xr",
    "c1xd",
    "c1xc",
    "d1r",
    "d1d",
    "d1c",
    "d1xr",
    "d1xd",
    "d1xc",
    "ma2f",
    "ma2g",
    "ma2o",
    "ma2xf",
    "ma2xg",
    "ma2xo",
    "mb2f",
    "mb2g",
    "mb2o",
    "mb2xf",
    "mb2xg",
    "mb2xo",
    "loc5",
    "rz0",
    "rz1",
    "sz0",
    "sz1",
    "at0",
    "at1",
    "at2",
    "pro",
)
STAGE = {name: number for number, name in enumerate(STAGES)}


def nt_dot(left, right, precision=None):
    return lax.dot_general(
        left, right, (((1,), (1,)), ((), ())), preferred_element_type=F32, precision=precision
    )


def row_sums(values):
    ones = jnp.ones((8, values.shape[1]), F32)
    return nt_dot(ones, values * values, HIGH)


def to_column(rows):
    size = rows.shape[1]
    eye = (
        lax.broadcasted_iota(jnp.int32, (size, size), 0)
        == lax.broadcasted_iota(jnp.int32, (size, size), 1)
    ).astype(F32)
    return nt_dot(eye, rows, HIGH)[:, :1]


def kernel(
    lens,
    hid_h,
    st_h,
    cache_h,
    gain1,
    wg_h,
    wi_h,
    wrt,
    rate_bias,
    decay_log,
    skip_gain,
    mix_gain,
    wio_h,
    wm_h,
    gain2,
    wq_h,
    wkv_h,
    wo_h,
    out,
    hid,
    nrm,
    wg,
    wi,
    wm,
    wq,
    wo,
    wio,
    kvw,
    st1,
    st2,
    ca1,
    ca2,
    accg,
    acci,
    accr,
    nio,
    iop,
    ior,
    iog,
    sq,
    gm,
    part,
    ra1,
    rb1,
    rja,
    rjb,
    qa,
    qb,
    ra2,
    rb2,
    rzs,
    rzr,
    res,
    sq2,
    sqy,
    mid,
    qs,
    qr,
    kvp,
    kvr,
    kvg,
    scores,
    os,
    orr,
    att,
    part2,
    rc1,
    rd1,
    rjc,
    rjd,
    qc,
    qd,
    rc2,
    rd2,
    szs,
    szr,
    fin,
    fo,
    fi,
    plain,
    sraw,
    stage,
    stw,
    craw,
    cwide,
    cw,
    ssem,
    rsem,
    psem,
):
    s = lax.axis_index("sample")
    t = lax.axis_index("tensor")
    z = lax.div(s, 16)
    y = lax.rem(lax.div(s, 4), 4)
    x = lax.rem(s, 4)
    g = lax.div(s, 4)
    i = 2 * x + t

    def al(value, size):
        return pl.multiple_of(value, size)

    def dev(sample, tensor):
        return {"sample": sample, "tensor": tensor}

    def dev_big_x(j):
        return dev(4 * g + lax.div(j, 2), lax.rem(j, 2))

    def dev_big_y(j):
        return dev(4 * j + x, t)

    def dev_x(j):
        return dev(4 * g + j, t)

    def dev_y(j):
        return dev(16 * z + 4 * j + x, t)

    sibling = dev(s, 1 - t)
    zpeer = dev(16 * (1 - z) + 4 * y + x, t)

    def remote(src, dst, stage, device, landing=None):
        return pltpu.make_async_remote_copy(
            src_ref=src,
            dst_ref=dst,
            send_sem=ssem.at[STAGE[stage]],
            recv_sem=rsem.at[STAGE[landing or stage]],
            device_id=device,
            device_id_type=MESH,
        )

    def local(src, dst, stage):
        return pltpu.make_async_copy(src, dst, rsem.at[STAGE[stage]])

    def all_sent(ref, stage):
        pltpu.make_async_copy(ref, ref, ssem.at[STAGE[stage]]).wait()

    pending = {}
    finish = []

    def exchange(stage, size, me, device, src_of, dst_of, span, own=False):
        def send(k, _):
            j = lax.rem(me + k, size)
            remote(src_of(j), dst_of(me), stage, device(j)).start()
            return 0

        if own:
            local(src_of(me), dst_of(me), stage).start()
        lax.fori_loop(1, size, send, 0)
        landed = span(size if own else size - 1)
        left = span(size - 1)
        pending[stage] = local(landed, landed, stage).wait
        finish.append(lambda: all_sent(left, stage))

    def swap(stage, src, dst, device):
        copy = remote(src, dst, stage, device)
        copy.start()
        pending[stage] = copy.wait_recv
        finish.append(copy.wait_send)

    def ring_start(stage, me, device, half, buf):
        right, left, far = (lax.rem(me + k, 4) for k in (1, 3, 2))
        remote(half(far, 0), buf.at[0], stage, device(right), stage + "r").start()
        remote(half(far, 1), buf.at[1], stage, device(left), stage + "r").start()
        remote(half(right, 1), buf.at[2], stage, device(right), stage + "d").start()
        remote(half(left, 0), buf.at[3], stage, device(left), stage + "d").start()
        for n, part_name in enumerate("rdc"):
            landed = buf.at[pl.ds(2 * n, 2)]
            pending[stage + part_name] = local(landed, landed, stage + part_name).wait

    def ring_pass(stage, me, device, half, buf, joined):
        right, left = lax.rem(me + 1, 4), lax.rem(me + 3, 4)
        arrive(stage + "r")
        joined[0] = (half(right, 0)[...].astype(F32) + buf[0].astype(F32)).astype(BF16)
        remote(joined.at[0], buf.at[4], stage, device(right), stage + "c").start()
        joined[1] = (half(left, 1)[...].astype(F32) + buf[1].astype(F32)).astype(BF16)
        remote(joined.at[1], buf.at[5], stage, device(left), stage + "c").start()
        finish.append(lambda: all_sent(buf, stage))

    def ring_total(stage, me, half, buf):
        arrive(stage + "d", stage + "c")
        return [
            half(me, h)[...].astype(F32) + buf[3 - h].astype(F32) + buf[4 + h].astype(F32)
            for h in range(2)
        ]

    def spread_start(stage, me, device, half):
        right, left = device(lax.rem(me + 1, 4)), device(lax.rem(me + 3, 4))
        remote(half(me, 0), half(me, 0), stage, right, stage + "f").start()
        remote(half(me, 1), half(me, 1), stage, left, stage + "f").start()
        remote(half(me, 1), half(me, 1), stage, right, stage + "g").start()
        remote(half(me, 0), half(me, 0), stage, left, stage + "g").start()

    def spread_pass(stage, me, device, half, span):
        right, left = lax.rem(me + 1, 4), lax.rem(me + 3, 4)
        one = span(1)
        local(one, one, stage + "f").wait()
        remote(half(left, 0), half(left, 0), stage, device(right), stage + "o").start()
        remote(half(right, 1), half(right, 1), stage, device(left), stage + "o").start()
        pending[stage + "g"] = local(one, one, stage + "g").wait
        pending[stage + "o"] = local(one, one, stage + "o").wait
        everything = span(3)
        finish.append(lambda: all_sent(everything, stage))

    def fetch(stage, src, dst):
        copy = local(src, dst, stage)
        copy.start()
        pending[stage] = copy.wait

    def arrive(*names):
        for name in names:
            pending.pop(name)()

    def drain():
        for name in list(pending):
            arrive(name)
        for wait in finish:
            wait()

    fetch("loc4", cache_h, craw)
    fetch("loc5", st_h, sraw)
    fetch("loc0", hid_h, hid)

    def proj_copy(c, src, dst, slot):
        rows = pl.ds(al(c * 2048, 2048), 2048)
        return pltpu.make_async_copy(src.at[rows], dst.at[rows], psem.at[2 * c + slot])

    def start_proj(c, _):
        proj_copy(c, wg_h, wg, 0).start()
        proj_copy(c, wi_h, wi, 1).start()
        return 0

    lax.fori_loop(0, 4, start_proj, 0)

    def project_wait(c, _):
        proj_copy(c, wg_h, wg, 0).wait()
        proj_copy(c, wi_h, wi, 1).wait()
        return 0

    pending["pro"] = lambda: lax.fori_loop(0, 4, project_wait, 0)

    barrier = pltpu.get_barrier_semaphore()
    me = 2 * s + t

    def greet(k, _):
        j = lax.rem(me + k, 64)
        pl.semaphore_signal(
            barrier, inc=1, device_id=dev(lax.div(j, 2), lax.rem(j, 2)), device_id_type=MESH
        )
        return 0

    lax.fori_loop(1, 64, greet, 0)
    arrive("loc4")
    cache_rows = craw[...].astype(F32).reshape(384, 256)
    for side in range(2):
        lanes = slice(128 * side, 128 * side + 128)
        cwide[side] = cache_rows[:, lanes]
        for j in range(8):
            picked = cwide[side, pl.ds(j, 48, stride=8), :]
            cw[j, :, :, lanes] = picked.astype(BF16).reshape(3, 16, 128)

    pl.semaphore_wait(barrier, 63)

    def wio_src(j):
        return wio_h.at[:, pl.ds(al(512 * j, 512), 512)]

    exchange("ca1", 8, g, dev_big_y, lambda j: cw.at[j], lambda j: ca1.at[:, j], lambda n: ca1.at[:, pl.ds(0, n)], own=True)
    exchange("wio", 8, g, dev_big_y, wio_src, lambda j: wio.at[j], lambda n: wio.at[pl.ds(0, n)], own=True)

    half = al(4096 * t, 4096)
    other = al(4096 * (1 - t), 4096)
    own_rows = pl.ds(al(256 * t, 256), 256)
    head_rows = pl.ds(al(128 * t, 128), 128)
    fetch("loc1", wm_h.at[:, pl.ds(half, 4096)], wm.at[own_rows])
    swap("w0", wm_h.at[:, pl.ds(other, 4096)], wm.at[own_rows], sibling)
    fetch("loc2", wq_h.at[pl.ds(half, 4096)], wq.at[:, head_rows])
    swap("w1", wq_h.at[pl.ds(other, 4096)], wq.at[:, head_rows], sibling)
    fetch("loc3", wo_h.at[:, pl.ds(half, 4096)], wo.at[head_rows])
    swap("w2", wo_h.at[:, pl.ds(other, 4096)], wo.at[head_rows], sibling)

    stage[...] = jnp.zeros_like(stage)
    line = lax.broadcasted_iota(jnp.int32, (256, 256), 0)
    block_of = lax.rem(line, 64)
    head_of = 32 * lax.rem(block_of, 8) + 4 * lax.div(block_of, 8) + lax.div(line, 64)
    pick_head = (head_of == lax.broadcasted_iota(jnp.int32, (256, 256), 1)).astype(F32).astype(BF16)
    arrive("loc5")
    for p in range(3):
        for n in range(4):
            turned = nt_dot(pick_head, sraw[p, :, n, :].astype(BF16))
            for side in range(2):
                stage[side, pl.ds(4 * p + n, 64, stride=16), :] = jnp.concatenate(
                    [turned[128 * side : 128 * side + 64], turned[128 * side + 64 : 128 * side + 128]],
                    axis=1,
                )
    for side in range(2):
        stw[:, :, :, 128 * side : 128 * side + 128] = (
            stage[side].astype(BF16).reshape(8, 8, 16, 128)
        )
    exchange("st1", 8, i, dev_big_x, lambda j: stw.at[j], lambda j: st1.at[j], lambda n: st1.at[pl.ds(0, n)], own=True)

    arrive("loc0")

    def norm_rows(r, _):
        rows = pl.ds(al(16 * r, 16), 16)
        values = hid[rows, :].astype(F32)
        scale = lax.rsqrt(jnp.mean(values * values, axis=1, keepdims=True) + 1e-05)
        nrm[rows, :] = (values * scale * gain1[...]).astype(BF16)
        return 0

    lax.fori_loop(0, 12, norm_rows, 0)
    arrive("ca1")
    exchange("ca2", 4, x, dev_x, lambda j: ca1, lambda j: ca2.at[j], lambda n: ca2.at[pl.ds(0, n)], own=True)

    accg[...] = jnp.zeros_like(accg)
    acci[...] = jnp.zeros_like(acci)
    accr[...] = jnp.zeros_like(accr)

    pending.pop("pro")

    def project(c, _):
        project_wait(c, 0)
        span = pl.ds(al(c * 2048, 2048), 2048)
        left = nrm[:, span]
        accg[...] += jnp.dot(left, wg[span, :], preferred_element_type=F32)
        acci[...] += jnp.dot(left, wi[span, :], preferred_element_type=F32)
        accr[...] += nt_dot(left, wrt[:, span])
        return 0

    lax.fori_loop(0, 4, project, 0)

    def pick(c, _):
        nio[:, pl.ds(al(128 * c, 128), 128)] = nrm[:, pl.ds(al(128 * (8 * c + i), 128), 128)]
        return 0

    lax.fori_loop(0, 8, pick, 0)
    arrive("wio", "st1")
    exchange("st2", 8, g, dev_big_y, lambda j: st1.at[:, j], lambda j: st2.at[j], lambda n: st2.at[pl.ds(0, n)], own=True)
    io_part = jnp.dot(nio[...], wio[...].reshape(1024, 512), preferred_element_type=F32)
    for j in range(8):
        iop[j] = io_part[24 * j : 24 * j + 24]
    exchange("iors", 8, i, dev_big_x, lambda j: iop.at[j], lambda j: ior.at[j], lambda n: ior.at[pl.ds(0, n)])
    arrive("iors")
    io_sum = iop[i].astype(F32)
    for k in range(1, 8):
        io_sum = io_sum + ior[lax.rem(i + k, 8)].astype(F32)
    iog[i] = io_sum.astype(BF16)
    exchange("ioag", 8, i, dev_big_x, lambda j: iog.at[i], lambda j: iog.at[j], lambda n: iog.at[pl.ds(0, n)])

    lift = (
        lax.broadcasted_iota(jnp.int32, (4, 256), 0)
        == lax.div(lax.broadcasted_iota(jnp.int32, (4, 256), 1), 64)
    ).astype(F32)

    def widen(heads):
        return jnp.dot(heads, lift, preferred_element_type=F32, precision=HIGH)

    raw = widen(accr[...] + rate_bias[...])
    rate = jnp.maximum(raw, 0.0) + jnp.log1p(jnp.exp(-jnp.abs(raw)))
    decay = jnp.exp(rate * -jnp.exp(widen(decay_log[...])))
    skip = widen(skip_gain[...])
    entering = rate * acci[...]
    column = lax.broadcasted_iota(jnp.int32, (256, 1024), 1)
    inside = lax.rem(column, 16)
    owner = lax.div(column, 16)
    spread = (
        (4 * owner + lax.rem(inside, 4) == lax.broadcasted_iota(jnp.int32, (256, 1024), 0))
        & (inside < 12)
    )
    spread = jnp.where(spread, 1.0, 0.0).astype(BF16)

    arrive("ioag")
    def kvw_src(j):
        return wkv_h.at[:, pl.ds(al(256 * j, 256), 256)]

    kvw_slot = 2 * y + t

    def kvw_copy(j, stage):
        return remote(kvw_src(j), kvw.at[kvw_slot], stage, dev(4 * j + x, z), "kvw")

    def kvw_send(k, _):
        kvw_copy(lax.rem(g + k, 8), "kvw").start()
        return 0

    lax.fori_loop(1, 8, kvw_send, 0)

    @pl.when(t == z)
    def _():
        local(kvw_src(g), kvw.at[kvw_slot], "kvw").start()

    @pl.when(t != z)
    def _():
        kvw_copy(g, "kvx").start()

    def kvw_finish():
        all_sent(kvw.at[pl.ds(0, 7)], "kvw")

        @pl.when(t != z)
        def _():
            kvw_copy(g, "kvx").wait_send()

    pending["kvw"] = local(kvw, kvw, "kvw").wait
    finish.append(kvw_finish)
    io_all = jnp.concatenate([iog[j].astype(F32) for j in range(8)], axis=0)
    in_vec = io_all[:, :256]
    out_vec = io_all[:, 256:]
    wide = jnp.dot(out_vec.astype(BF16), spread, preferred_element_type=F32)
    row_prompt = lax.rem(lax.div(lax.broadcasted_iota(jnp.int32, (192, 1024), 0), 16), 3)
    col_prompt = lax.div(
        lax.rem(lax.broadcasted_iota(jnp.int32, (192, 1024), 1), 16), 4
    )
    wide = jnp.where(row_prompt == col_prompt, wide, 0.0).astype(BF16)
    arrive("st2")
    start = jnp.dot(wide, st2[...].reshape(1024, 256), preferred_element_type=F32)

    mixed = []
    running = None
    carried = []
    for step in range(4):
        rows = slice(48 * step, 48 * step + 48)
        fall = decay[rows]
        running = fall if running is None else running * fall
        carried = [term * fall for term in carried] + [entering[rows]]
        value = running * start[rows]
        for earlier in range(step + 1):
            match = jnp.sum(
                out_vec[rows] * in_vec[48 * earlier : 48 * earlier + 48], axis=1, keepdims=True
            )
            value = value + match * carried[earlier]
        mixed.append(value + skip * acci[rows, :])
    gate = accg[...]
    gated = jnp.concatenate(mixed, axis=0) * (gate / (1.0 + jnp.exp(-gate)))
    gm[:, own_rows] = (gated * mix_gain[...]).astype(BF16)
    swap("gm", gm.at[:, own_rows], gm.at[:, own_rows], sibling)
    sq[i] = row_sums(gated)
    exchange("sq", 8, i, dev_big_x, lambda j: sq.at[i], lambda j: sq.at[j], lambda n: sq.at[pl.ds(0, n)])
    def mix_scale():
        arrive("sq")
        group_sum = sq[0]
        for j in range(1, 8):
            group_sum = group_sum + sq[j]
        return to_column(lax.rsqrt(group_sum * (1.0 / 2048.0) + 1e-05))

    arrive("gm", "loc1", "w0")

    my_rows = pl.ds(al(48 * y, 48), 48)
    low = pl.ds(0, 256)
    high = pl.ds(256, 256)

    def rows_of(j):
        return pl.ds(al(48 * j, 48), 48)

    def half_a(p, c):
        return lambda j, h: p.at[c, pl.ds(2 * h, 2), rows_of(j), low]

    def half_b(p, c):
        return lambda j, h: p.at[c, j, pl.ds(96 * h, 96), high]

    def reduce_scatter(names, left, weight, scaling, p, a1, b1, ja, jb, sa, sb, a2, b2, zs, zr, use):
        na1, nb1, na2, nb2, nz = names
        tails = ("", "x")
        scales = []

        for c in range(2):

            def block(n, _, c=c):
                xx = lax.div(n, 2)
                hh = lax.rem(n, 2)
                cols = pl.ds(al(1024 * xx + 512 * hh + 256 * c, 256), 256)
                value = jnp.dot(left[...], weight[:, cols], preferred_element_type=F32)
                if scaling is not None and c == 0:
                    plain[n] = value
                    return 0
                if scaling is not None:
                    value = value * scales[0]
                p[c, xx, :, pl.ds(al(256 * hh, 256), 256)] = value.astype(BF16)
                return 0

            lax.fori_loop(0, 8, block, 0, unroll=4)
            if scaling is not None and c == 0:
                scales.append(scaling())

                def rescale(n, _):
                    p[0, lax.div(n, 2), :, pl.ds(al(256 * lax.rem(n, 2), 256), 256)] = (
                        plain[n] * scales[0]
                    ).astype(BF16)
                    return 0

                lax.fori_loop(0, 8, rescale, 0)
            ring_start(na1 + tails[c], y, dev_y, half_a(p, c), a1.at[c])
            ring_start(nb1 + tails[c], x, dev_x, half_b(p, c), b1.at[c])
        for c in range(2):
            ring_pass(na1 + tails[c], y, dev_y, half_a(p, c), a1.at[c], ja.at[c])
            ring_pass(nb1 + tails[c], x, dev_x, half_b(p, c), b1.at[c], jb.at[c])
        for c in range(2):
            totals = ring_total(na1 + tails[c], y, half_a(p, c), a1.at[c])
            for h in range(2):
                sa[c, 2 * h : 2 * h + 2] = totals[h].astype(BF16)
            exchange(
                na2 + tails[c],
                4,
                x,
                dev_x,
                lambda j, c=c: sa.at[c, j],
                lambda j, c=c: a2.at[c, j],
                lambda n, c=c: a2.at[c, pl.ds(0, n)],
            )
            totals = ring_total(nb1 + tails[c], x, half_b(p, c), b1.at[c])
            for h in range(2):
                sb[c, 96 * h : 96 * h + 96, :] = totals[h].astype(BF16)
            exchange(
                nb2 + tails[c],
                4,
                y,
                dev_y,
                lambda j, c=c: sb.at[c, rows_of(j)],
                lambda j, c=c: b2.at[c, j],
                lambda n, c=c: b2.at[c, pl.ds(0, n)],
            )
        for c in range(2):
            arrive(na2 + tails[c])
            total = sa[c, x].astype(F32)
            for k in range(1, 4):
                total = total + a2[c, lax.rem(x + k, 4)].astype(F32)
            zs[c, :, 0:256] = total.astype(BF16)
            arrive(nb2 + tails[c])
            total = sb[c, my_rows, :].astype(F32)
            for k in range(1, 4):
                total = total + b2[c, lax.rem(y + k, 4)].astype(F32)
            zs[c, :, 256:512] = total.astype(BF16)
            swap(nz + str(c), zs.at[c], zr.at[c], zpeer)
        for c in range(2):
            arrive(nz + str(c))
            use(c, zs[c].astype(F32) + zr[c].astype(F32))

    feature = al(1024 * (4 * t + x), 1024)
    squares = []

    def use_mix(c, value):
        spans = [al(feature + 256 * c, 256), al(feature + 512 + 256 * c, 256)]
        old = jnp.concatenate([hid[my_rows, pl.ds(span, 256)] for span in spans], axis=1)
        gain = jnp.concatenate([gain2[:, pl.ds(span, 256)] for span in spans], axis=1)
        residual = old.astype(F32) + value
        res[c] = residual
        mid[c, x, my_rows, :] = (residual * gain).astype(BF16)
        tail = ("", "x")[c]
        exchange(
            "ma1" + tail,
            4,
            x,
            dev_x,
            lambda j: mid.at[c, x, my_rows, low],
            lambda j: mid.at[c, j, my_rows, low],
            lambda n: mid.at[c, pl.ds(0, n), my_rows, low],
        )
        exchange(
            "mb1" + tail,
            4,
            y,
            dev_y,
            lambda j: mid.at[c, x, my_rows, high],
            lambda j: mid.at[c, x, rows_of(j), high],
            lambda n: mid.at[c, x, pl.ds(0, 48 * n), high],
        )
        squares.append(row_sums(residual))

    reduce_scatter(
        ("a1", "b1", "a2", "b2", "rz"),
        gm,
        wm,
        mix_scale,
        part,
        ra1,
        rb1,
        rja,
        rjb,
        qa,
        qb,
        ra2,
        rb2,
        rzs,
        rzr,
        use_mix,
    )
    sq2[i] = squares[0] + squares[1]
    exchange("sq2", 8, i, dev_big_x, lambda j: sq2.at[i], lambda j: sq2.at[j], lambda n: sq2.at[pl.ds(0, n)])
    for c in range(2):
        tail = ("", "x")[c]
        arrive("ma1" + tail)
        spread_start("ma2" + tail, y, dev_y, half_a(mid, c))
        arrive("mb1" + tail)
        spread_start("mb2" + tail, x, dev_x, half_b(mid, c))
    for c in range(2):
        tail = ("", "x")[c]
        spread_pass(
            "ma2" + tail,
            y,
            dev_y,
            half_a(mid, c),
            lambda n, c=c: mid.at[c, :, pl.ds(0, 48 * n), low],
        )
        spread_pass(
            "mb2" + tail, x, dev_x, half_b(mid, c), lambda n, c=c: mid.at[c, pl.ds(0, n), :, high]
        )
    arrive("sq2")
    row_sum = sq2[0]
    for j in range(1, 8):
        row_sum = row_sum + sq2[j]
    sqy[y] = row_sum
    exchange("sqy", 4, y, dev_y, lambda j: sqy.at[y], lambda j: sqy.at[j], lambda n: sqy.at[pl.ds(0, n)])
    arrive("sqy")
    scale = jnp.concatenate(
        [to_column(lax.rsqrt(sqy[j] * (1.0 / 8192.0) + 1e-05)) for j in range(4)], axis=0
    )

    arrive("loc2", "w1", "kvw")
    query = jnp.zeros((192, 256), F32)
    pair = jnp.zeros((192, 256), F32)
    for c in range(2):
        tail = ("", "x")[c]
        for name in ("ma2", "mb2"):
            arrive(name + tail + "g", name + tail + "o")
        for xx in range(4):
            for hh in range(2):
                place = 1024 * xx + 512 * hh + 256 * c
                query = query + jnp.dot(
                    mid[c, xx, :, 256 * hh : 256 * hh + 256],
                    wq[place : place + 256, :],
                    preferred_element_type=F32,
                )
    for xx in range(4):
        pair = pair + jnp.dot(
            mid[lax.rem(x, 2), xx, :, pl.ds(al(256 * lax.div(x, 2), 256), 256)],
            kvw[2 * xx : 2 * xx + 2].reshape(256, 256),
            preferred_element_type=F32,
        )
    pair = pair * scale
    for j in range(8):
        kvp[j] = pair[24 * j : 24 * j + 24]
    exchange("kvr", 8, i, dev_big_x, lambda j: kvp.at[j], lambda j: kvr.at[j], lambda n: kvr.at[pl.ds(0, n)])
    qs[...] = query
    swap("q", qs, qr, sibling)

    arrive("kvr")
    pair_sum = kvp[i].astype(F32)
    for k in range(1, 8):
        pair_sum = pair_sum + kvr[lax.rem(i + k, 8)].astype(F32)
    kvg[i] = pair_sum.astype(BF16)
    exchange("kva", 8, i, dev_big_x, lambda j: kvg.at[i], lambda j: kvg.at[j], lambda n: kvg.at[pl.ds(0, n)])

    arrive("q")
    query_rows = ((qs[...] + qr[...]) * (scale * (128.0**-0.5))).astype(BF16)
    arrive("ca2")
    query_of = []
    lane = lax.broadcasted_iota(jnp.int32, (128, 128), 1)
    place = 128 * lax.div(lane, 16) + lax.rem(lane, 16) + 16 * t
    for p in range(3):
        query_p = jnp.concatenate(
            [
                query_rows[48 * step + 16 * p : 48 * step + 16 * p + 16, 128 * head : 128 * head + 128]
                for head in range(2)
                for step in range(4)
            ],
            axis=0,
        )
        query_of.append(query_p)
        for j in range(4):
            keys = ca2[j, p, :, :, 0:128].reshape(128, 128)
            score = nt_dot(query_p, keys)
            scores[p, :, 128 * j : 128 * j + 128] = jnp.where(
                place + 32 * j < lens[p], score, -1e30
            )

    arrive("kva")
    pair_all = jnp.concatenate([kvg[j].astype(F32) for j in range(8)], axis=0)
    row_step = lax.rem(lax.div(lax.broadcasted_iota(jnp.int32, (128, 1), 0), 16), 4)
    row_step = row_step - 4 * t
    wide_lane = lax.broadcasted_iota(jnp.int32, (128, 128), 1)
    for p in range(3):
        far = scores[p]
        top = jnp.max(far, axis=1, keepdims=True)
        near = []
        values = []
        query_p = query_of[p].astype(F32)
        for step in range(4):
            block = pair_all[48 * step + 16 * p : 48 * step + 16 * p + 16]
            tiled = jnp.concatenate([block] * 8, axis=0)
            values.append(tiled[:, 128:])
            score = jnp.sum(query_p * tiled[:, :128], axis=1, keepdims=True)
            score = jnp.where(row_step >= step, score, -1e30)
            near.append(score)
            top = jnp.maximum(top, score)
        far = jnp.exp(far - top)
        near = [jnp.exp(score - top) for score in near]
        total = jnp.sum(far, axis=1, keepdims=True)
        for weight in near:
            total = total + weight
        far = far.astype(BF16)
        result = jnp.zeros((128, 128), F32)
        for j in range(4):
            result = result + jnp.dot(
                far[:, 128 * j : 128 * j + 128],
                ca2[j, p, :, :, 128:256].reshape(128, 128),
                preferred_element_type=F32,
            )
        for weight, value in zip(near, values):
            result = result + weight.astype(BF16).astype(F32) * value
        os[p, :, 0:128] = result
        os[p, :, 128:256] = jnp.where(wide_lane < 64, top, total)
        swap("at" + str(p), os.at[p], orr.at[p], sibling)
    for p in range(3):
        arrive("at" + str(p))
        mine_top, mine_total = os[p, :, 128:129], os[p, :, 192:193]
        peer_top, peer_total = orr[p, :, 128:129], orr[p, :, 192:193]
        top = jnp.maximum(mine_top, peer_top)
        mine = jnp.exp(mine_top - top)
        peer = jnp.exp(peer_top - top)
        total = mine_total * mine + peer_total * peer
        result = (os[p, :, 0:128] * (mine / total) + orr[p, :, 0:128] * (peer / total)).astype(BF16)
        for head in range(2):
            for step in range(4):
                att[48 * step + 16 * p : 48 * step + 16 * p + 16, 128 * head : 128 * head + 128] = (
                    result[64 * head + 16 * step : 64 * head + 16 * step + 16]
                )

    arrive("loc3", "w2")

    def use_out(c, value):
        value = res[c] + value
        fin[0:48, 256 * c : 256 * c + 256] = value[:, 0:256]
        fin[0:48, 512 + 256 * c : 768 + 256 * c] = value[:, 256:512]

    reduce_scatter(
        ("c1", "d1", "c2", "d2", "sz"),
        att,
        wo,
        None,
        part2,
        rc1,
        rd1,
        rjc,
        rjd,
        qc,
        qd,
        rc2,
        rd2,
        szs,
        szr,
        use_out,
    )

    fin[48:56, :] = jnp.zeros((8, 1024), F32)
    sends = lax.div(y, 2) == z

    def fin_copy(k):
        target = 16 * y + k
        return remote(fo.at[k], fi.at[i], "fin", dev(lax.div(target, 2), lax.rem(target, 2)))

    @pl.when(sends)
    def _():
        for k in range(16):
            fo[k] = fin[3 * k : 3 * k + 8, :].astype(BF16)

        def send(k, _):
            @pl.when(16 * y + k == me)
            def _():
                local(fo.at[k], fi.at[i], "fin").start()

            @pl.when(16 * y + k != me)
            def _():
                fin_copy(k).start()

            return 0

        lax.fori_loop(0, 16, send, 0)

    keeps = sends & (lax.div(me, 16) == y)

    def fin_finish():
        @pl.when(keeps)
        def _():
            all_sent(fo.at[pl.ds(0, 15)], "fin")

        @pl.when(sends & (lax.div(me, 16) != y))
        def _():
            all_sent(fo, "fin")

    local(fi, fi, "fin").wait()
    finish.append(fin_finish)
    for j in range(8):
        place_j = 1024 * (4 * (j % 2) + j // 2)
        out[:, place_j : place_j + 1024] = fi[j][0:3, :]
    drain()


def scratch():
    def v(shape, dtype=BF16):
        return pltpu.VMEM(shape, dtype)

    reduce_bufs = [
        v((2, 6, 2, 48, 256)),
        v((2, 6, 96, 256)),
        v((2, 2, 2, 48, 256)),
        v((2, 2, 96, 256)),
        v((2, 4, 48, 256)),
        v((2, 192, 256)),
        v((2, 4, 48, 256)),
        v((2, 4, 48, 256)),
        v((2, 48, 512)),
        v((2, 48, 512)),
    ]
    return [
        v((192, 8192)),
        v((192, 8192)),
        v((8192, 256)),
        v((8192, 256)),
        v((512, 4096)),
        v((4096, 256)),
        v((256, 4096)),
        v((8, 128, 512)),
        v((8, 128, 256)),
        v((8, 8, 16, 256)),
        v((8, 8, 16, 256)),
        v((3, 8, 16, 256)),
        v((4, 3, 8, 16, 256)),
        v((192, 256), F32),
        v((192, 256), F32),
        v((192, 4), F32),
        v((192, 1024)),
        v((8, 24, 512), F32),
        v((8, 24, 512), F32),
        v((8, 24, 512)),
        v((8, 8, 192), F32),
        v((192, 512)),
        v((2, 4, 192, 512)),
        *reduce_bufs,
        v((2, 48, 512), F32),
        v((8, 8, 48), F32),
        v((4, 8, 48), F32),
        v((2, 4, 192, 512)),
        v((192, 256), F32),
        v((192, 256), F32),
        v((8, 24, 256), F32),
        v((8, 24, 256), F32),
        v((8, 24, 256)),
        v((3, 128, 512), F32),
        v((3, 128, 256), F32),
        v((3, 128, 256), F32),
        v((192, 256)),
        v((2, 4, 192, 512)),
        *reduce_bufs,
        v((56, 1024), F32),
        v((16, 8, 1024)),
        v((8, 8, 1024)),
        v((8, 192, 256), F32),
        v((3, 64, 4, 256), F32),
        v((2, 1024, 128), F32),
        v((8, 8, 16, 256)),
        v((3, 16, 8, 256)),
        v((2, 384, 128), F32),
        v((8, 3, 16, 256)),
        pltpu.SemaphoreType.DMA((len(STAGES),)),
        pltpu.SemaphoreType.DMA((len(STAGES),)),
        pltpu.SemaphoreType.DMA((8,)),
    ]


def shards(
    hidden_input,
    prompt_lengths,
    prompt_states,
    prompt_cache,
    input_gain,
    gate_weight,
    input_weight,
    rate_weight,
    rate_bias,
    decay_log,
    skip_gain,
    state_io_weight,
    mix_gain,
    mix_weight,
    middle_gain,
    query_weight,
    key_value_weight,
    output_weight,
):
    hidden = hidden_input.reshape(192, 8192)
    states = prompt_states.transpose(0, 2, 3, 1)
    vmem = pl.BlockSpec(memory_space=pltpu.VMEM)
    smem = pl.BlockSpec(memory_space=pltpu.SMEM)
    anyw = pl.BlockSpec(memory_space=pl.ANY)
    return pl.pallas_call(
        kernel,
        out_shape=jax.ShapeDtypeStruct((3, 8192), BF16),
        in_specs=[
            smem,
            anyw,
            anyw,
            anyw,
            vmem,
            anyw,
            anyw,
            vmem,
            vmem,
            vmem,
            vmem,
            vmem,
            anyw,
            anyw,
            vmem,
            anyw,
            anyw,
            anyw,
        ],
        out_specs=vmem,
        scratch_shapes=scratch(),
        compiler_params=pltpu.CompilerParams(
            collective_id=0, has_side_effects=True, vmem_limit_bytes=60 * 1024 * 1024
        ),
        cost_estimate=pl.CostEstimate(
            flops=4_000_000_000, bytes_accessed=24_000_000, transcendentals=1_000_000
        ),
    )(
        prompt_lengths,
        hidden,
        states,
        prompt_cache,
        input_gain[None, :],
        gate_weight,
        input_weight,
        rate_weight.T,
        rate_bias[None, :],
        decay_log[None, :],
        skip_gain[None, :],
        mix_gain[None, :],
        state_io_weight,
        mix_weight,
        middle_gain[None, :],
        query_weight,
        key_value_weight,
        output_weight,
    )


def solution(mesh):
    in_specs = (
        P(None, "prompt", None),
        P("prompt"),
        P("prompt", None, None, ("sample", "tensor")),
        P("prompt", ("sample", "tensor"), None, None),
        P(),
        P(None, ("sample", "tensor")),
        P(None, ("sample", "tensor")),
        P(None, ("sample", "tensor")),
        P(("sample", "tensor")),
        P(("sample", "tensor")),
        P(("sample", "tensor")),
        P(("sample", "tensor"), None),
        P(("sample", "tensor")),
        P(("sample", "tensor"), None),
        P(),
        P(None, ("sample", "tensor")),
        P(("sample", "tensor"), None),
        P(("sample", "tensor"), None),
    )
    out_specs = P(("prompt", "sample", "tensor"), None)
    return jax.shard_map(shards, mesh=mesh, in_specs=in_specs, out_specs=out_specs, check_vma=False)
```

```python
import jax
import jax.numpy as jnp
from jax import lax
from jax.experimental import pallas as pl
from jax.experimental.pallas import tpu as pltpu
from jax.sharding import PartitionSpec as P

F32 = jnp.float32
BF16 = jnp.bfloat16
MESH = pl.DeviceIdType.MESH
HIGH = lax.Precision.HIGHEST

SENDS, LANDINGS = 51, 80


def nt_dot(left, right, precision=None):
    return lax.dot_general(
        left, right, (((1,), (1,)), ((), ())), preferred_element_type=F32, precision=precision
    )


def row_sums(values):
    ones = jnp.ones((8, values.shape[1]), F32)
    return nt_dot(ones, values * values, HIGH)


def to_column(rows):
    size = rows.shape[1]
    eye = (
        lax.broadcasted_iota(jnp.int32, (size, size), 0)
        == lax.broadcasted_iota(jnp.int32, (size, size), 1)
    ).astype(F32)
    return nt_dot(eye, rows, HIGH)[:, :1]


def kernel(
    lens,
    hid_h,
    st_h,
    cache_h,
    gain1,
    wg_h,
    wi_h,
    wrt,
    rate_bias,
    decay_log,
    skip_gain,
    mix_gain,
    wio_h,
    wm_h,
    gain2,
    wq_h,
    wkv_h,
    wo_h,
    out,
    hid,
    nrm,
    wg,
    wi,
    wm,
    wq,
    wo,
    wio,
    kvw,
    st1,
    st2,
    ca1,
    ca2,
    accg,
    acci,
    accr,
    nio,
    iop,
    ior,
    iog,
    sq,
    gm,
    part,
    ra1,
    rb1,
    rja,
    rjb,
    qa,
    qb,
    ra2,
    rb2,
    rzs,
    rzr,
    res,
    sq2,
    sqy,
    mid,
    qs,
    qr,
    kvp,
    kvr,
    kvg,
    scores,
    os,
    orr,
    att,
    part2,
    rc1,
    rd1,
    rjc,
    rjd,
    qc,
    qd,
    rc2,
    rd2,
    szs,
    szr,
    fin,
    fo,
    fi,
    plain,
    sraw,
    stage,
    stw,
    craw,
    cwide,
    cw,
    ssem,
    rsem,
    psem,
):
    s = lax.axis_index("sample")
    t = lax.axis_index("tensor")
    z = lax.div(s, 16)
    y = lax.rem(lax.div(s, 4), 4)
    x = lax.rem(s, 4)
    g = lax.div(s, 4)
    i = 2 * x + t

    def al(value, size):
        return pl.multiple_of(value, size)

    def dev(sample, tensor):
        return {"sample": sample, "tensor": tensor}

    def dev_big_x(j):
        return dev(4 * g + lax.div(j, 2), lax.rem(j, 2))

    def dev_big_y(j):
        return dev(4 * j + x, t)

    def dev_x(j):
        return dev(4 * g + j, t)

    def dev_y(j):
        return dev(16 * z + 4 * j + x, t)

    sibling = dev(s, 1 - t)
    zpeer = dev(16 * (1 - z) + 4 * y + x, t)

    sends_of, landings_of = {}, {}

    def number(table, stage):
        return table.setdefault(stage, len(table))

    def remote(src, dst, stage, device, landing=None):
        return pltpu.make_async_remote_copy(
            src_ref=src,
            dst_ref=dst,
            send_sem=ssem.at[number(sends_of, stage)],
            recv_sem=rsem.at[number(landings_of, landing or stage)],
            device_id=device,
            device_id_type=MESH,
        )

    def local(src, dst, stage):
        return pltpu.make_async_copy(src, dst, rsem.at[number(landings_of, stage)])

    def all_sent(ref, stage):
        pltpu.make_async_copy(ref, ref, ssem.at[number(sends_of, stage)]).wait()

    pending = {}
    finish = []

    def exchange(stage, size, me, device, src_of, dst_of, span, own=False):
        def send(k, _):
            j = lax.rem(me + k, size)
            remote(src_of(j), dst_of(me), stage, device(j)).start()
            return 0

        if own:
            local(src_of(me), dst_of(me), stage).start()
        lax.fori_loop(1, size, send, 0)
        landed = span(size if own else size - 1)
        left = span(size - 1)
        pending[stage] = local(landed, landed, stage).wait
        finish.append(lambda: all_sent(left, stage))

    def swap(stage, src, dst, device):
        copy = remote(src, dst, stage, device)
        copy.start()
        pending[stage] = copy.wait_recv
        finish.append(copy.wait_send)

    def ring_start(stage, me, device, half, buf):
        right, left, far = (lax.rem(me + k, 4) for k in (1, 3, 2))
        remote(half(far, 0), buf.at[0], stage, device(right), stage + "r").start()
        remote(half(far, 1), buf.at[1], stage, device(left), stage + "r").start()
        remote(half(right, 1), buf.at[2], stage, device(right), stage + "d").start()
        remote(half(left, 0), buf.at[3], stage, device(left), stage + "d").start()
        for n, part_name in enumerate("rdc"):
            landed = buf.at[pl.ds(2 * n, 2)]
            pending[stage + part_name] = local(landed, landed, stage + part_name).wait

    def ring_pass(stage, me, device, half, buf, joined):
        right, left = lax.rem(me + 1, 4), lax.rem(me + 3, 4)
        arrive(stage + "r")
        joined[0] = (half(right, 0)[...].astype(F32) + buf[0].astype(F32)).astype(BF16)
        remote(joined.at[0], buf.at[4], stage, device(right), stage + "c").start()
        joined[1] = (half(left, 1)[...].astype(F32) + buf[1].astype(F32)).astype(BF16)
        remote(joined.at[1], buf.at[5], stage, device(left), stage + "c").start()
        finish.append(lambda: all_sent(buf, stage))

    def ring_total(stage, me, half, buf):
        arrive(stage + "d", stage + "c")
        return [
            half(me, h)[...].astype(F32) + buf[3 - h].astype(F32) + buf[4 + h].astype(F32)
            for h in range(2)
        ]

    def spread_start(stage, me, device, half):
        right, left = device(lax.rem(me + 1, 4)), device(lax.rem(me + 3, 4))
        remote(half(me, 0), half(me, 0), stage, right, stage + "f").start()
        remote(half(me, 1), half(me, 1), stage, left, stage + "f").start()
        remote(half(me, 1), half(me, 1), stage, right, stage + "g").start()
        remote(half(me, 0), half(me, 0), stage, left, stage + "g").start()

    def spread_pass(stage, me, device, half, span):
        right, left = lax.rem(me + 1, 4), lax.rem(me + 3, 4)
        one = span(1)
        local(one, one, stage + "f").wait()
        remote(half(left, 0), half(left, 0), stage, device(right), stage + "o").start()
        remote(half(right, 1), half(right, 1), stage, device(left), stage + "o").start()
        pending[stage + "g"] = local(one, one, stage + "g").wait
        pending[stage + "o"] = local(one, one, stage + "o").wait
        everything = span(3)
        finish.append(lambda: all_sent(everything, stage))

    def fetch(stage, src, dst):
        copy = local(src, dst, stage)
        copy.start()
        pending[stage] = copy.wait

    def arrive(*names):
        for name in names:
            pending.pop(name)()

    def drain():
        for name in list(pending):
            arrive(name)
        for wait in finish:
            wait()

    fetch("loc4", cache_h, craw)
    fetch("loc5", st_h, sraw)
    fetch("loc0", hid_h, hid)

    def proj_copy(c, src, dst, slot):
        rows = pl.ds(al(c * 2048, 2048), 2048)
        return pltpu.make_async_copy(src.at[rows], dst.at[rows], psem.at[2 * c + slot])

    def start_proj(c, _):
        proj_copy(c, wg_h, wg, 0).start()
        proj_copy(c, wi_h, wi, 1).start()
        return 0

    lax.fori_loop(0, 4, start_proj, 0)

    def project_wait(c, _):
        proj_copy(c, wg_h, wg, 0).wait()
        proj_copy(c, wi_h, wi, 1).wait()
        return 0

    pending["pro"] = lambda: lax.fori_loop(0, 4, project_wait, 0)

    barrier = pltpu.get_barrier_semaphore()
    me = 2 * s + t

    def greet(k, _):
        j = lax.rem(me + k, 64)
        pl.semaphore_signal(
            barrier, inc=1, device_id=dev(lax.div(j, 2), lax.rem(j, 2)), device_id_type=MESH
        )
        return 0

    lax.fori_loop(1, 64, greet, 0)
    arrive("loc4")
    cache_rows = craw[...].astype(F32).reshape(384, 256)
    for side in range(2):
        lanes = slice(128 * side, 128 * side + 128)
        cwide[side] = cache_rows[:, lanes]
        for j in range(8):
            picked = cwide[side, pl.ds(j, 48, stride=8), :]
            cw[j, :, :, lanes] = picked.astype(BF16).reshape(3, 16, 128)

    pl.semaphore_wait(barrier, 63)

    def wio_src(j):
        return wio_h.at[:, pl.ds(al(512 * j, 512), 512)]

    exchange("ca1", 8, g, dev_big_y, lambda j: cw.at[j], lambda j: ca1.at[:, j], lambda n: ca1.at[:, pl.ds(0, n)], own=True)
    exchange("wio", 8, g, dev_big_y, wio_src, lambda j: wio.at[j], lambda n: wio.at[pl.ds(0, n)], own=True)

    half = al(4096 * t, 4096)
    other = al(4096 * (1 - t), 4096)
    own_rows = pl.ds(al(256 * t, 256), 256)
    head_rows = pl.ds(al(128 * t, 128), 128)
    fetch("loc1", wm_h.at[:, pl.ds(half, 4096)], wm.at[own_rows])
    swap("w0", wm_h.at[:, pl.ds(other, 4096)], wm.at[own_rows], sibling)
    fetch("loc2", wq_h.at[pl.ds(half, 4096)], wq.at[:, head_rows])
    swap("w1", wq_h.at[pl.ds(other, 4096)], wq.at[:, head_rows], sibling)
    fetch("loc3", wo_h.at[:, pl.ds(half, 4096)], wo.at[head_rows])
    swap("w2", wo_h.at[:, pl.ds(other, 4096)], wo.at[head_rows], sibling)

    stage[...] = jnp.zeros_like(stage)
    line = lax.broadcasted_iota(jnp.int32, (256, 256), 0)
    block_of = lax.rem(line, 64)
    head_of = 32 * lax.rem(block_of, 8) + 4 * lax.div(block_of, 8) + lax.div(line, 64)
    pick_head = (head_of == lax.broadcasted_iota(jnp.int32, (256, 256), 1)).astype(F32).astype(BF16)
    arrive("loc5")
    for p in range(3):
        for n in range(4):
            turned = nt_dot(pick_head, sraw[p, :, n, :].astype(BF16))
            for side in range(2):
                stage[side, pl.ds(4 * p + n, 64, stride=16), :] = jnp.concatenate(
                    [turned[128 * side : 128 * side + 64], turned[128 * side + 64 : 128 * side + 128]],
                    axis=1,
                )
    for side in range(2):
        stw[:, :, :, 128 * side : 128 * side + 128] = (
            stage[side].astype(BF16).reshape(8, 8, 16, 128)
        )
    exchange("st1", 8, i, dev_big_x, lambda j: stw.at[j], lambda j: st1.at[j], lambda n: st1.at[pl.ds(0, n)], own=True)

    arrive("loc0")

    def norm_rows(r, _):
        rows = pl.ds(al(16 * r, 16), 16)
        values = hid[rows, :].astype(F32)
        scale = lax.rsqrt(jnp.mean(values * values, axis=1, keepdims=True) + 1e-05)
        nrm[rows, :] = (values * scale * gain1[...]).astype(BF16)
        return 0

    lax.fori_loop(0, 12, norm_rows, 0)
    arrive("ca1")
    exchange("ca2", 4, x, dev_x, lambda j: ca1, lambda j: ca2.at[j], lambda n: ca2.at[pl.ds(0, n)], own=True)

    accg[...] = jnp.zeros_like(accg)
    acci[...] = jnp.zeros_like(acci)
    accr[...] = jnp.zeros_like(accr)

    pending.pop("pro")

    def project(c, _):
        project_wait(c, 0)
        span = pl.ds(al(c * 2048, 2048), 2048)
        left = nrm[:, span]
        accg[...] += jnp.dot(left, wg[span, :], preferred_element_type=F32)
        acci[...] += jnp.dot(left, wi[span, :], preferred_element_type=F32)
        accr[...] += nt_dot(left, wrt[:, span])
        return 0

    lax.fori_loop(0, 4, project, 0)

    def pick(c, _):
        nio[:, pl.ds(al(128 * c, 128), 128)] = nrm[:, pl.ds(al(128 * (8 * c + i), 128), 128)]
        return 0

    lax.fori_loop(0, 8, pick, 0)
    arrive("wio", "st1")
    io_part = jnp.dot(nio[...], wio[...].reshape(1024, 512), preferred_element_type=F32)
    for j in range(8):
        iop[j] = io_part[24 * j : 24 * j + 24]
    exchange("iors", 8, i, dev_big_x, lambda j: iop.at[j], lambda j: ior.at[j], lambda n: ior.at[pl.ds(0, n)])
    exchange("st2", 8, g, dev_big_y, lambda j: st1.at[:, j], lambda j: st2.at[j], lambda n: st2.at[pl.ds(0, n)], own=True)
    arrive("iors")
    io_sum = iop[i].astype(F32)
    for k in range(1, 8):
        io_sum = io_sum + ior[lax.rem(i + k, 8)].astype(F32)
    iog[i] = io_sum.astype(BF16)
    exchange("ioag", 8, i, dev_big_x, lambda j: iog.at[i], lambda j: iog.at[j], lambda n: iog.at[pl.ds(0, n)])

    lift = (
        lax.broadcasted_iota(jnp.int32, (4, 256), 0)
        == lax.div(lax.broadcasted_iota(jnp.int32, (4, 256), 1), 64)
    ).astype(F32)

    def widen(heads):
        return jnp.dot(heads, lift, preferred_element_type=F32, precision=HIGH)

    raw = widen(accr[...] + rate_bias[...])
    rate = jnp.maximum(raw, 0.0) + jnp.log1p(jnp.exp(-jnp.abs(raw)))
    decay = jnp.exp(rate * -jnp.exp(widen(decay_log[...])))
    skip = widen(skip_gain[...])
    entering = rate * acci[...]
    column = lax.broadcasted_iota(jnp.int32, (256, 1024), 1)
    inside = lax.rem(column, 16)
    owner = lax.div(column, 16)
    spread = (
        (4 * owner + lax.rem(inside, 4) == lax.broadcasted_iota(jnp.int32, (256, 1024), 0))
        & (inside < 12)
    )
    spread = jnp.where(spread, 1.0, 0.0).astype(BF16)

    arrive("ioag")
    def kvw_src(j):
        return wkv_h.at[:, pl.ds(al(256 * j, 256), 256)]

    kvw_slot = 2 * y + t

    def kvw_copy(j, stage):
        return remote(kvw_src(j), kvw.at[kvw_slot], stage, dev(4 * j + x, z), "kvw")

    def kvw_send(k, _):
        kvw_copy(lax.rem(g + k, 8), "kvw").start()
        return 0

    lax.fori_loop(1, 8, kvw_send, 0)

    @pl.when(t == z)
    def _():
        local(kvw_src(g), kvw.at[kvw_slot], "kvw").start()

    @pl.when(t != z)
    def _():
        kvw_copy(g, "kvx").start()

    def kvw_finish():
        all_sent(kvw.at[pl.ds(0, 7)], "kvw")

        @pl.when(t != z)
        def _():
            kvw_copy(g, "kvx").wait_send()

    pending["kvw"] = local(kvw, kvw, "kvw").wait
    finish.append(kvw_finish)
    io_all = jnp.concatenate([iog[j].astype(F32) for j in range(8)], axis=0)
    in_vec = io_all[:, :256]
    out_vec = io_all[:, 256:]
    wide = jnp.dot(out_vec.astype(BF16), spread, preferred_element_type=F32)
    row_prompt = lax.rem(lax.div(lax.broadcasted_iota(jnp.int32, (192, 1024), 0), 16), 3)
    col_prompt = lax.div(
        lax.rem(lax.broadcasted_iota(jnp.int32, (192, 1024), 1), 16), 4
    )
    wide = jnp.where(row_prompt == col_prompt, wide, 0.0).astype(BF16)
    arrive("st2")
    start = jnp.dot(wide, st2[...].reshape(1024, 256), preferred_element_type=F32)

    mixed = []
    running = None
    carried = []
    for step in range(4):
        rows = slice(48 * step, 48 * step + 48)
        fall = decay[rows]
        running = fall if running is None else running * fall
        carried = [term * fall for term in carried] + [entering[rows]]
        value = running * start[rows]
        for earlier in range(step + 1):
            match = jnp.sum(
                out_vec[rows] * in_vec[48 * earlier : 48 * earlier + 48], axis=1, keepdims=True
            )
            value = value + match * carried[earlier]
        mixed.append(value + skip * acci[rows, :])
    gate = accg[...]
    gated = jnp.concatenate(mixed, axis=0) * (gate / (1.0 + jnp.exp(-gate)))
    gm[:, own_rows] = (gated * mix_gain[...]).astype(BF16)
    swap("gm", gm.at[:, own_rows], gm.at[:, own_rows], sibling)
    sq[i] = row_sums(gated)
    exchange("sq", 8, i, dev_big_x, lambda j: sq.at[i], lambda j: sq.at[j], lambda n: sq.at[pl.ds(0, n)])
    def mix_scale():
        arrive("sq")
        group_sum = sq[0]
        for j in range(1, 8):
            group_sum = group_sum + sq[j]
        return to_column(lax.rsqrt(group_sum * (1.0 / 2048.0) + 1e-05))

    arrive("gm", "loc1", "w0")

    my_rows = pl.ds(al(48 * y, 48), 48)
    low = pl.ds(0, 256)
    high = pl.ds(256, 256)

    def rows_of(j):
        return pl.ds(al(48 * j, 48), 48)

    def half_a(p, c):
        return lambda j, h: p.at[c, pl.ds(2 * h, 2), rows_of(j), low]

    def half_b(p, c):
        return lambda j, h: p.at[c, j, pl.ds(96 * h, 96), high]

    def reduce_scatter(names, left, weight, scaling, p, a1, b1, ja, jb, sa, sb, a2, b2, zs, zr, use):
        na1, nb1, na2, nb2, nz = names
        tails = ("", "x")
        scales = []

        for c in range(2):

            for hh in (1, 0):

                def block(xx, _, c=c, hh=hh):
                    cols = pl.ds(al(1024 * xx + 512 * hh + 256 * c, 256), 256)
                    value = jnp.dot(left[...], weight[:, cols], preferred_element_type=F32)
                    if scaling is not None and c == 0 and hh == 1:
                        plain[xx] = value
                        return 0
                    if scaling is not None:
                        value = value * scales[0]
                    p[c, xx, :, 256 * hh : 256 * hh + 256] = value.astype(BF16)
                    return 0

                lax.fori_loop(0, 4, block, 0, unroll=4)
                if scaling is not None and c == 0 and hh == 1:
                    scales.append(scaling())

                    def rescale(xx, _):
                        p[0, xx, :, 256:512] = (plain[xx] * scales[0]).astype(BF16)
                        return 0

                    lax.fori_loop(0, 4, rescale, 0)
                if hh == 1:
                    ring_start(nb1 + tails[c], x, dev_x, half_b(p, c), b1.at[c])
                else:
                    ring_start(na1 + tails[c], y, dev_y, half_a(p, c), a1.at[c])
        for c in range(2):
            ring_pass(na1 + tails[c], y, dev_y, half_a(p, c), a1.at[c], ja.at[c])
            ring_pass(nb1 + tails[c], x, dev_x, half_b(p, c), b1.at[c], jb.at[c])
        for c in range(2):
            totals = ring_total(na1 + tails[c], y, half_a(p, c), a1.at[c])
            for h in range(2):
                sa[c, 2 * h : 2 * h + 2] = totals[h].astype(BF16)
            exchange(
                na2 + tails[c],
                4,
                x,
                dev_x,
                lambda j, c=c: sa.at[c, j],
                lambda j, c=c: a2.at[c, j],
                lambda n, c=c: a2.at[c, pl.ds(0, n)],
            )
            totals = ring_total(nb1 + tails[c], x, half_b(p, c), b1.at[c])
            for h in range(2):
                sb[c, 96 * h : 96 * h + 96, :] = totals[h].astype(BF16)
            exchange(
                nb2 + tails[c],
                4,
                y,
                dev_y,
                lambda j, c=c: sb.at[c, rows_of(j)],
                lambda j, c=c: b2.at[c, j],
                lambda n, c=c: b2.at[c, pl.ds(0, n)],
            )
        for c in range(2):
            arrive(na2 + tails[c])
            total = sa[c, x].astype(F32)
            for k in range(1, 4):
                total = total + a2[c, lax.rem(x + k, 4)].astype(F32)
            zs[c, :, 0:256] = total.astype(BF16)
            arrive(nb2 + tails[c])
            total = sb[c, my_rows, :].astype(F32)
            for k in range(1, 4):
                total = total + b2[c, lax.rem(y + k, 4)].astype(F32)
            zs[c, :, 256:512] = total.astype(BF16)
            swap(nz + str(c), zs.at[c], zr.at[c], zpeer)
        for c in range(2):
            arrive(nz + str(c))
            use(c, zs[c].astype(F32) + zr[c].astype(F32))

    feature = al(1024 * (4 * t + x), 1024)
    squares = []

    def use_mix(c, value):
        spans = [al(feature + 256 * c, 256), al(feature + 512 + 256 * c, 256)]
        old = jnp.concatenate([hid[my_rows, pl.ds(span, 256)] for span in spans], axis=1)
        gain = jnp.concatenate([gain2[:, pl.ds(span, 256)] for span in spans], axis=1)
        residual = old.astype(F32) + value
        res[c] = residual
        mid[c, x, my_rows, :] = (residual * gain).astype(BF16)
        tail = ("", "x")[c]
        exchange(
            "ma1" + tail,
            4,
            x,
            dev_x,
            lambda j: mid.at[c, x, my_rows, low],
            lambda j: mid.at[c, j, my_rows, low],
            lambda n: mid.at[c, pl.ds(0, n), my_rows, low],
        )
        exchange(
            "mb1" + tail,
            4,
            y,
            dev_y,
            lambda j: mid.at[c, x, my_rows, high],
            lambda j: mid.at[c, x, rows_of(j), high],
            lambda n: mid.at[c, x, pl.ds(0, 48 * n), high],
        )
        squares.append(row_sums(residual))

    reduce_scatter(
        ("a1", "b1", "a2", "b2", "rz"),
        gm,
        wm,
        mix_scale,
        part,
        ra1,
        rb1,
        rja,
        rjb,
        qa,
        qb,
        ra2,
        rb2,
        rzs,
        rzr,
        use_mix,
    )
    sq2[i] = squares[0] + squares[1]
    exchange("sq2", 8, i, dev_big_x, lambda j: sq2.at[i], lambda j: sq2.at[j], lambda n: sq2.at[pl.ds(0, n)])
    for c in range(2):
        tail = ("", "x")[c]
        arrive("ma1" + tail)
        spread_start("ma2" + tail, y, dev_y, half_a(mid, c))
        arrive("mb1" + tail)
        spread_start("mb2" + tail, x, dev_x, half_b(mid, c))
    for c in range(2):
        tail = ("", "x")[c]
        spread_pass(
            "ma2" + tail,
            y,
            dev_y,
            half_a(mid, c),
            lambda n, c=c: mid.at[c, :, pl.ds(0, 48 * n), low],
        )
        spread_pass(
            "mb2" + tail, x, dev_x, half_b(mid, c), lambda n, c=c: mid.at[c, pl.ds(0, n), :, high]
        )
    arrive("sq2")
    row_sum = sq2[0]
    for j in range(1, 8):
        row_sum = row_sum + sq2[j]
    sqy[y] = row_sum
    exchange("sqy", 4, y, dev_y, lambda j: sqy.at[y], lambda j: sqy.at[j], lambda n: sqy.at[pl.ds(0, n)])
    arrive("loc2", "w1", "kvw")
    query = jnp.zeros((192, 256), F32)
    pair = jnp.zeros((192, 256), F32)
    for c in range(2):
        tail = ("", "x")[c]
        for name in ("ma2", "mb2"):
            arrive(name + tail + "g", name + tail + "o")
        if c == 1:
            for xx in range(4):
                pair = pair + jnp.dot(
                    mid[lax.rem(x, 2), xx, :, pl.ds(al(256 * lax.div(x, 2), 256), 256)],
                    kvw[2 * xx : 2 * xx + 2].reshape(256, 256),
                    preferred_element_type=F32,
                )
            arrive("sqy")
            scale = jnp.concatenate(
                [to_column(lax.rsqrt(sqy[j] * (1.0 / 8192.0) + 1e-05)) for j in range(4)], axis=0
            )
            pair = pair * scale
            for j in range(8):
                kvp[j] = pair[24 * j : 24 * j + 24]
            exchange(
                "kvr",
                8,
                i,
                dev_big_x,
                lambda j: kvp.at[j],
                lambda j: kvr.at[j],
                lambda n: kvr.at[pl.ds(0, n)],
            )
        for xx in range(4):
            for hh in range(2):
                place = 1024 * xx + 512 * hh + 256 * c
                query = query + jnp.dot(
                    mid[c, xx, :, 256 * hh : 256 * hh + 256],
                    wq[place : place + 256, :],
                    preferred_element_type=F32,
                )
    qs[...] = query
    swap("q", qs, qr, sibling)

    arrive("kvr")
    pair_sum = kvp[i].astype(F32)
    for k in range(1, 8):
        pair_sum = pair_sum + kvr[lax.rem(i + k, 8)].astype(F32)
    kvg[i] = pair_sum.astype(BF16)
    exchange("kva", 8, i, dev_big_x, lambda j: kvg.at[i], lambda j: kvg.at[j], lambda n: kvg.at[pl.ds(0, n)])

    arrive("q")
    query_rows = ((qs[...] + qr[...]) * (scale * (128.0**-0.5))).astype(BF16)
    arrive("ca2")
    query_of = []
    lane = lax.broadcasted_iota(jnp.int32, (128, 128), 1)
    place = 128 * lax.div(lane, 16) + lax.rem(lane, 16) + 16 * t
    for p in range(3):
        query_p = jnp.concatenate(
            [
                query_rows[48 * step + 16 * p : 48 * step + 16 * p + 16, 128 * head : 128 * head + 128]
                for head in range(2)
                for step in range(4)
            ],
            axis=0,
        )
        query_of.append(query_p)
        for j in range(4):
            keys = ca2[j, p, :, :, 0:128].reshape(128, 128)
            score = nt_dot(query_p, keys)
            scores[p, :, 128 * j : 128 * j + 128] = jnp.where(
                place + 32 * j < lens[p], score, -1e30
            )

    arrive("kva")
    pair_all = jnp.concatenate([kvg[j].astype(F32) for j in range(8)], axis=0)
    row_step = lax.rem(lax.div(lax.broadcasted_iota(jnp.int32, (128, 1), 0), 16), 4)
    row_step = row_step - 4 * t
    wide_lane = lax.broadcasted_iota(jnp.int32, (128, 128), 1)
    for p in range(3):
        far = scores[p]
        top = jnp.max(far, axis=1, keepdims=True)
        near = []
        values = []
        query_p = query_of[p].astype(F32)
        for step in range(4):
            block = pair_all[48 * step + 16 * p : 48 * step + 16 * p + 16]
            tiled = jnp.concatenate([block] * 8, axis=0)
            values.append(tiled[:, 128:])
            score = jnp.sum(query_p * tiled[:, :128], axis=1, keepdims=True)
            score = jnp.where(row_step >= step, score, -1e30)
            near.append(score)
            top = jnp.maximum(top, score)
        far = jnp.exp(far - top)
        near = [jnp.exp(score - top) for score in near]
        total = jnp.sum(far, axis=1, keepdims=True)
        for weight in near:
            total = total + weight
        far = far.astype(BF16)
        result = jnp.zeros((128, 128), F32)
        for j in range(4):
            result = result + jnp.dot(
                far[:, 128 * j : 128 * j + 128],
                ca2[j, p, :, :, 128:256].reshape(128, 128),
                preferred_element_type=F32,
            )
        for weight, value in zip(near, values):
            result = result + weight.astype(BF16).astype(F32) * value
        os[p, :, 0:128] = result
        os[p, :, 128:256] = jnp.where(wide_lane < 64, top, total)
        swap("at" + str(p), os.at[p], orr.at[p], sibling)
    for p in range(3):
        arrive("at" + str(p))
        mine_top, mine_total = os[p, :, 128:129], os[p, :, 192:193]
        peer_top, peer_total = orr[p, :, 128:129], orr[p, :, 192:193]
        top = jnp.maximum(mine_top, peer_top)
        mine = jnp.exp(mine_top - top)
        peer = jnp.exp(peer_top - top)
        total = mine_total * mine + peer_total * peer
        result = (os[p, :, 0:128] * (mine / total) + orr[p, :, 0:128] * (peer / total)).astype(BF16)
        for head in range(2):
            for step in range(4):
                att[48 * step + 16 * p : 48 * step + 16 * p + 16, 128 * head : 128 * head + 128] = (
                    result[64 * head + 16 * step : 64 * head + 16 * step + 16]
                )

    arrive("loc3", "w2")

    def use_out(c, value):
        value = res[c] + value
        fin[0:48, 256 * c : 256 * c + 256] = value[:, 0:256]
        fin[0:48, 512 + 256 * c : 768 + 256 * c] = value[:, 256:512]

    reduce_scatter(
        ("c1", "d1", "c2", "d2", "sz"),
        att,
        wo,
        None,
        part2,
        rc1,
        rd1,
        rjc,
        rjd,
        qc,
        qd,
        rc2,
        rd2,
        szs,
        szr,
        use_out,
    )

    fin[48:56, :] = jnp.zeros((8, 1024), F32)
    sends = lax.div(y, 2) == z

    def fin_copy(k):
        target = 16 * y + k
        return remote(fo.at[k], fi.at[i], "fin", dev(lax.div(target, 2), lax.rem(target, 2)))

    @pl.when(sends)
    def _():
        for k in range(16):
            fo[k] = fin[3 * k : 3 * k + 8, :].astype(BF16)

        def send(k, _):
            @pl.when(16 * y + k == me)
            def _():
                local(fo.at[k], fi.at[i], "fin").start()

            @pl.when(16 * y + k != me)
            def _():
                fin_copy(k).start()

            return 0

        lax.fori_loop(0, 16, send, 0)

    keeps = sends & (lax.div(me, 16) == y)

    def fin_finish():
        @pl.when(keeps)
        def _():
            all_sent(fo.at[pl.ds(0, 15)], "fin")

        @pl.when(sends & (lax.div(me, 16) != y))
        def _():
            all_sent(fo, "fin")

    local(fi, fi, "fin").wait()
    finish.append(fin_finish)
    for j in range(8):
        place_j = 1024 * (4 * (j % 2) + j // 2)
        out[:, place_j : place_j + 1024] = fi[j][0:3, :]
    drain()


def scratch():
    def v(shape, dtype=BF16):
        return pltpu.VMEM(shape, dtype)

    reduce_bufs = [
        v((2, 6, 2, 48, 256)),
        v((2, 6, 96, 256)),
        v((2, 2, 2, 48, 256)),
        v((2, 2, 96, 256)),
        v((2, 4, 48, 256)),
        v((2, 192, 256)),
        v((2, 4, 48, 256)),
        v((2, 4, 48, 256)),
        v((2, 48, 512)),
        v((2, 48, 512)),
    ]
    return [
        v((192, 8192)),
        v((192, 8192)),
        v((8192, 256)),
        v((8192, 256)),
        v((512, 4096)),
        v((4096, 256)),
        v((256, 4096)),
        v((8, 128, 512)),
        v((8, 128, 256)),
        v((8, 8, 16, 256)),
        v((8, 8, 16, 256)),
        v((3, 8, 16, 256)),
        v((4, 3, 8, 16, 256)),
        v((192, 256), F32),
        v((192, 256), F32),
        v((192, 4), F32),
        v((192, 1024)),
        v((8, 24, 512), F32),
        v((8, 24, 512), F32),
        v((8, 24, 512)),
        v((8, 8, 192), F32),
        v((192, 512)),
        v((2, 4, 192, 512)),
        *reduce_bufs,
        v((2, 48, 512), F32),
        v((8, 8, 48), F32),
        v((4, 8, 48), F32),
        v((2, 4, 192, 512)),
        v((192, 256), F32),
        v((192, 256), F32),
        v((8, 24, 256), F32),
        v((8, 24, 256), F32),
        v((8, 24, 256)),
        v((3, 128, 512), F32),
        v((3, 128, 256), F32),
        v((3, 128, 256), F32),
        v((192, 256)),
        v((2, 4, 192, 512)),
        *reduce_bufs,
        v((56, 1024), F32),
        v((16, 8, 1024)),
        v((8, 8, 1024)),
        v((4, 192, 256), F32),
        v((3, 64, 4, 256), F32),
        v((2, 1024, 128), F32),
        v((8, 8, 16, 256)),
        v((3, 16, 8, 256)),
        v((2, 384, 128), F32),
        v((8, 3, 16, 256)),
        pltpu.SemaphoreType.DMA((SENDS,)),
        pltpu.SemaphoreType.DMA((LANDINGS,)),
        pltpu.SemaphoreType.DMA((8,)),
    ]


def shards(
    hidden_input,
    prompt_lengths,
    prompt_states,
    prompt_cache,
    input_gain,
    gate_weight,
    input_weight,
    rate_weight,
    rate_bias,
    decay_log,
    skip_gain,
    state_io_weight,
    mix_gain,
    mix_weight,
    middle_gain,
    query_weight,
    key_value_weight,
    output_weight,
):
    hidden = hidden_input.reshape(192, 8192)
    states = prompt_states.transpose(0, 2, 3, 1)
    vmem = pl.BlockSpec(memory_space=pltpu.VMEM)
    smem = pl.BlockSpec(memory_space=pltpu.SMEM)
    anyw = pl.BlockSpec(memory_space=pl.ANY)
    return pl.pallas_call(
        kernel,
        out_shape=jax.ShapeDtypeStruct((3, 8192), BF16),
        in_specs=[
            smem,
            anyw,
            anyw,
            anyw,
            vmem,
            anyw,
            anyw,
            vmem,
            vmem,
            vmem,
            vmem,
            vmem,
            anyw,
            anyw,
            vmem,
            anyw,
            anyw,
            anyw,
        ],
        out_specs=vmem,
        scratch_shapes=scratch(),
        compiler_params=pltpu.CompilerParams(
            collective_id=0, has_side_effects=True, vmem_limit_bytes=60 * 1024 * 1024
        ),
        cost_estimate=pl.CostEstimate(
            flops=4_000_000_000, bytes_accessed=24_000_000, transcendentals=1_000_000
        ),
    )(
        prompt_lengths,
        hidden,
        states,
        prompt_cache,
        input_gain[None, :],
        gate_weight,
        input_weight,
        rate_weight.T,
        rate_bias[None, :],
        decay_log[None, :],
        skip_gain[None, :],
        mix_gain[None, :],
        state_io_weight,
        mix_weight,
        middle_gain[None, :],
        query_weight,
        key_value_weight,
        output_weight,
    )


def solution(mesh):
    in_specs = (
        P(None, "prompt", None),
        P("prompt"),
        P("prompt", None, None, ("sample", "tensor")),
        P("prompt", ("sample", "tensor"), None, None),
        P(),
        P(None, ("sample", "tensor")),
        P(None, ("sample", "tensor")),
        P(None, ("sample", "tensor")),
        P(("sample", "tensor")),
        P(("sample", "tensor")),
        P(("sample", "tensor")),
        P(("sample", "tensor"), None),
        P(("sample", "tensor")),
        P(("sample", "tensor"), None),
        P(),
        P(None, ("sample", "tensor")),
        P(("sample", "tensor"), None),
        P(("sample", "tensor"), None),
    )
    out_specs = P(("prompt", "sample", "tensor"), None)
    return jax.shard_map(shards, mesh=mesh, in_specs=in_specs, out_specs=out_specs, check_vma=False)
```

```python
import jax
import jax.numpy as jnp
from jax import lax
from jax.experimental import pallas as pl
from jax.experimental.pallas import tpu as pltpu
from jax.sharding import PartitionSpec as P

F32 = jnp.float32
BF16 = jnp.bfloat16
MESH = pl.DeviceIdType.MESH
HIGH = lax.Precision.HIGHEST

SENDS, LANDINGS = 51, 80


def nt_dot(left, right, precision=None):
    return lax.dot_general(
        left, right, (((1,), (1,)), ((), ())), preferred_element_type=F32, precision=precision
    )


def row_sums(values):
    ones = jnp.ones((8, values.shape[1]), F32)
    return nt_dot(ones, values * values, HIGH)


def to_column(rows):
    size = rows.shape[1]
    eye = (
        lax.broadcasted_iota(jnp.int32, (size, size), 0)
        == lax.broadcasted_iota(jnp.int32, (size, size), 1)
    ).astype(F32)
    return nt_dot(eye, rows, HIGH)[:, :1]


def kernel(
    lens,
    hid_h,
    st_h,
    cache_h,
    gain1,
    wg_h,
    wi_h,
    wrt,
    rate_bias,
    decay_log,
    skip_gain,
    mix_gain,
    wio_h,
    wm_h,
    gain2,
    wq_h,
    wkv_h,
    wo_h,
    out,
    hid,
    nrm,
    wg,
    wi,
    wm,
    wq,
    wo,
    wio,
    kvw,
    st1,
    st2,
    ca1,
    ca2,
    accg,
    acci,
    accr,
    nio,
    iop,
    ior,
    iog,
    sq,
    gm,
    part,
    ra1,
    rb1,
    rja,
    rjb,
    qa,
    qb,
    ra2,
    rb2,
    rzs,
    rzr,
    res,
    sq2,
    sqy,
    mid,
    qs,
    qr,
    kvp,
    kvr,
    kvg,
    scores,
    os,
    orr,
    att,
    part2,
    rc1,
    rd1,
    rjc,
    rjd,
    qc,
    qd,
    rc2,
    rd2,
    szs,
    szr,
    fin,
    fo,
    fi,
    plain,
    sraw,
    stage,
    stw,
    craw,
    cwide,
    cw,
    ssem,
    rsem,
    psem,
):
    s = lax.axis_index("sample")
    t = lax.axis_index("tensor")
    z = lax.div(s, 16)
    y = lax.rem(lax.div(s, 4), 4)
    x = lax.rem(s, 4)
    g = lax.div(s, 4)
    i = 2 * x + t

    def al(value, size):
        return pl.multiple_of(value, size)

    def dev(sample, tensor):
        return {"sample": sample, "tensor": tensor}

    def dev_big_x(j):
        return dev(4 * g + lax.div(j, 2), lax.rem(j, 2))

    def dev_big_y(j):
        return dev(4 * j + x, t)

    def dev_x(j):
        return dev(4 * g + j, t)

    def dev_y(j):
        return dev(16 * z + 4 * j + x, t)

    sibling = dev(s, 1 - t)
    zpeer = dev(16 * (1 - z) + 4 * y + x, t)

    sends_of, landings_of = {}, {}

    def number(table, stage):
        return table.setdefault(stage, len(table))

    def remote(src, dst, stage, device, landing=None):
        return pltpu.make_async_remote_copy(
            src_ref=src,
            dst_ref=dst,
            send_sem=ssem.at[number(sends_of, stage)],
            recv_sem=rsem.at[number(landings_of, landing or stage)],
            device_id=device,
            device_id_type=MESH,
        )

    def local(src, dst, stage):
        return pltpu.make_async_copy(src, dst, rsem.at[number(landings_of, stage)])

    def all_sent(ref, stage):
        pltpu.make_async_copy(ref, ref, ssem.at[number(sends_of, stage)]).wait()

    pending = {}
    finish = []

    def exchange(stage, size, me, device, src_of, dst_of, span, own=False):
        def send(k, _):
            j = lax.rem(me + k, size)
            remote(src_of(j), dst_of(me), stage, device(j)).start()
            return 0

        if own:
            local(src_of(me), dst_of(me), stage).start()
        lax.fori_loop(1, size, send, 0)
        landed = span(size if own else size - 1)
        left = span(size - 1)
        pending[stage] = local(landed, landed, stage).wait
        finish.append(lambda: all_sent(left, stage))

    def swap(stage, src, dst, device):
        copy = remote(src, dst, stage, device)
        copy.start()
        pending[stage] = copy.wait_recv
        finish.append(copy.wait_send)

    def ring_start(stage, me, device, half, buf):
        right, left, far = (lax.rem(me + k, 4) for k in (1, 3, 2))
        remote(half(far, 0), buf.at[0], stage, device(right), stage + "r").start()
        remote(half(far, 1), buf.at[1], stage, device(left), stage + "r").start()
        remote(half(right, 1), buf.at[2], stage, device(right), stage + "d").start()
        remote(half(left, 0), buf.at[3], stage, device(left), stage + "d").start()
        for n, part_name in enumerate("rdc"):
            landed = buf.at[pl.ds(2 * n, 2)]
            pending[stage + part_name] = local(landed, landed, stage + part_name).wait

    def ring_pass(stage, me, device, half, buf, joined):
        right, left = lax.rem(me + 1, 4), lax.rem(me + 3, 4)
        arrive(stage + "r")
        joined[0] = (half(right, 0)[...].astype(F32) + buf[0].astype(F32)).astype(BF16)
        remote(joined.at[0], buf.at[4], stage, device(right), stage + "c").start()
        joined[1] = (half(left, 1)[...].astype(F32) + buf[1].astype(F32)).astype(BF16)
        remote(joined.at[1], buf.at[5], stage, device(left), stage + "c").start()
        finish.append(lambda: all_sent(buf, stage))

    def ring_total(stage, me, half, buf):
        arrive(stage + "d", stage + "c")
        return [
            half(me, h)[...].astype(F32) + buf[3 - h].astype(F32) + buf[4 + h].astype(F32)
            for h in range(2)
        ]

    def spread_start(stage, me, device, half):
        right, left = device(lax.rem(me + 1, 4)), device(lax.rem(me + 3, 4))
        remote(half(me, 0), half(me, 0), stage, right, stage + "f").start()
        remote(half(me, 1), half(me, 1), stage, left, stage + "f").start()
        remote(half(me, 1), half(me, 1), stage, right, stage + "g").start()
        remote(half(me, 0), half(me, 0), stage, left, stage + "g").start()

    def spread_pass(stage, me, device, half, span):
        right, left = lax.rem(me + 1, 4), lax.rem(me + 3, 4)
        one = span(1)
        local(one, one, stage + "f").wait()
        remote(half(left, 0), half(left, 0), stage, device(right), stage + "o").start()
        remote(half(right, 1), half(right, 1), stage, device(left), stage + "o").start()
        pending[stage + "g"] = local(one, one, stage + "g").wait
        pending[stage + "o"] = local(one, one, stage + "o").wait
        everything = span(3)
        finish.append(lambda: all_sent(everything, stage))

    def fetch(stage, src, dst):
        copy = local(src, dst, stage)
        copy.start()
        pending[stage] = copy.wait

    def arrive(*names):
        for name in names:
            pending.pop(name)()

    def drain():
        for name in list(pending):
            arrive(name)
        for wait in finish:
            wait()

    fetch("loc4", cache_h, craw)
    fetch("loc5", st_h, sraw)
    fetch("loc0", hid_h, hid)

    def proj_copy(c, src, dst, slot):
        rows = pl.ds(al(c * 2048, 2048), 2048)
        return pltpu.make_async_copy(src.at[rows], dst.at[rows], psem.at[2 * c + slot])

    def start_proj(c, _):
        proj_copy(c, wg_h, wg, 0).start()
        proj_copy(c, wi_h, wi, 1).start()
        return 0

    lax.fori_loop(0, 4, start_proj, 0)

    def project_wait(c, _):
        proj_copy(c, wg_h, wg, 0).wait()
        proj_copy(c, wi_h, wi, 1).wait()
        return 0

    pending["pro"] = lambda: lax.fori_loop(0, 4, project_wait, 0)

    barrier = pltpu.get_barrier_semaphore()
    me = 2 * s + t

    def greet(k, _):
        j = lax.rem(me + k, 64)
        pl.semaphore_signal(
            barrier, inc=1, device_id=dev(lax.div(j, 2), lax.rem(j, 2)), device_id_type=MESH
        )
        return 0

    lax.fori_loop(1, 64, greet, 0)
    arrive("loc4")
    cache_rows = craw[...].astype(F32).reshape(384, 256)
    for side in range(2):
        lanes = slice(128 * side, 128 * side + 128)
        cwide[side] = cache_rows[:, lanes]
        for j in range(8):
            picked = cwide[side, pl.ds(j, 48, stride=8), :]
            cw[j, :, :, lanes] = picked.astype(BF16).reshape(3, 16, 128)

    pl.semaphore_wait(barrier, 63)

    def wio_src(j):
        return wio_h.at[:, pl.ds(al(512 * j, 512), 512)]

    exchange("ca1", 8, g, dev_big_y, lambda j: cw.at[j], lambda j: ca1.at[:, j], lambda n: ca1.at[:, pl.ds(0, n)], own=True)
    exchange("wio", 8, g, dev_big_y, wio_src, lambda j: wio.at[j], lambda n: wio.at[pl.ds(0, n)], own=True)

    half = al(4096 * t, 4096)
    other = al(4096 * (1 - t), 4096)
    own_rows = pl.ds(al(256 * t, 256), 256)
    head_rows = pl.ds(al(128 * t, 128), 128)
    fetch("loc1", wm_h.at[:, pl.ds(half, 4096)], wm.at[own_rows])
    swap("w0", wm_h.at[:, pl.ds(other, 4096)], wm.at[own_rows], sibling)
    fetch("loc2", wq_h.at[pl.ds(half, 4096)], wq.at[:, head_rows])
    swap("w1", wq_h.at[pl.ds(other, 4096)], wq.at[:, head_rows], sibling)
    fetch("loc3", wo_h.at[:, pl.ds(half, 4096)], wo.at[head_rows])
    swap("w2", wo_h.at[:, pl.ds(other, 4096)], wo.at[head_rows], sibling)

    stage[...] = jnp.zeros_like(stage)
    line = lax.broadcasted_iota(jnp.int32, (256, 256), 0)
    block_of = lax.rem(line, 64)
    head_of = 32 * lax.rem(block_of, 8) + 4 * lax.div(block_of, 8) + lax.div(line, 64)
    pick_head = (head_of == lax.broadcasted_iota(jnp.int32, (256, 256), 1)).astype(F32).astype(BF16)
    arrive("loc5")
    for p in range(3):
        for n in range(4):
            turned = nt_dot(pick_head, sraw[p, :, n, :].astype(BF16))
            for side in range(2):
                stage[side, pl.ds(4 * p + n, 64, stride=16), :] = jnp.concatenate(
                    [turned[128 * side : 128 * side + 64], turned[128 * side + 64 : 128 * side + 128]],
                    axis=1,
                )
    for side in range(2):
        stw[:, :, :, 128 * side : 128 * side + 128] = (
            stage[side].astype(BF16).reshape(8, 8, 16, 128)
        )
    exchange("st1", 8, i, dev_big_x, lambda j: stw.at[j], lambda j: st1.at[j], lambda n: st1.at[pl.ds(0, n)], own=True)

    arrive("ca1")
    exchange("ca2", 4, x, dev_x, lambda j: ca1, lambda j: ca2.at[j], lambda n: ca2.at[pl.ds(0, n)], own=True)

    arrive("loc0")

    def norm_rows(r, _):
        rows = pl.ds(al(16 * r, 16), 16)
        values = hid[rows, :].astype(F32)
        scale = lax.rsqrt(jnp.mean(values * values, axis=1, keepdims=True) + 1e-05)
        nrm[rows, :] = (values * scale * gain1[...]).astype(BF16)
        return 0

    lax.fori_loop(0, 12, norm_rows, 0)

    accg[...] = jnp.zeros_like(accg)
    acci[...] = jnp.zeros_like(acci)
    accr[...] = jnp.zeros_like(accr)

    pending.pop("pro")

    def project(c, _):
        project_wait(c, 0)
        span = pl.ds(al(c * 2048, 2048), 2048)
        left = nrm[:, span]
        accg[...] += jnp.dot(left, wg[span, :], preferred_element_type=F32)
        acci[...] += jnp.dot(left, wi[span, :], preferred_element_type=F32)
        accr[...] += nt_dot(left, wrt[:, span])
        return 0

    lax.fori_loop(0, 4, project, 0)

    def pick(c, _):
        nio[:, pl.ds(al(128 * c, 128), 128)] = nrm[:, pl.ds(al(128 * (8 * c + i), 128), 128)]
        return 0

    lax.fori_loop(0, 8, pick, 0)
    arrive("wio", "st1")
    io_part = jnp.dot(nio[...], wio[...].reshape(1024, 512), preferred_element_type=F32)
    for j in range(8):
        iop[j] = io_part[24 * j : 24 * j + 24]
    exchange("iors", 8, i, dev_big_x, lambda j: iop.at[j], lambda j: ior.at[j], lambda n: ior.at[pl.ds(0, n)])
    exchange("st2", 8, g, dev_big_y, lambda j: st1.at[:, j], lambda j: st2.at[j], lambda n: st2.at[pl.ds(0, n)], own=True)

    def kvw_src(j):
        return wkv_h.at[:, pl.ds(al(256 * j, 256), 256)]

    kvw_slot = 2 * y + t

    def kvw_copy(j, stage):
        return remote(kvw_src(j), kvw.at[kvw_slot], stage, dev(4 * j + x, z), "kvw")

    def kvw_send(k, _):
        kvw_copy(lax.rem(g + k, 8), "kvw").start()
        return 0

    lax.fori_loop(1, 8, kvw_send, 0)

    @pl.when(t == z)
    def _():
        local(kvw_src(g), kvw.at[kvw_slot], "kvw").start()

    @pl.when(t != z)
    def _():
        kvw_copy(g, "kvx").start()

    def kvw_finish():
        all_sent(kvw.at[pl.ds(0, 7)], "kvw")

        @pl.when(t != z)
        def _():
            kvw_copy(g, "kvx").wait_send()

    pending["kvw"] = local(kvw, kvw, "kvw").wait
    finish.append(kvw_finish)

    arrive("iors")
    io_sum = iop[i].astype(F32)
    for k in range(1, 8):
        io_sum = io_sum + ior[lax.rem(i + k, 8)].astype(F32)
    iog[i] = io_sum.astype(BF16)
    exchange("ioag", 8, i, dev_big_x, lambda j: iog.at[i], lambda j: iog.at[j], lambda n: iog.at[pl.ds(0, n)])

    lift = (
        lax.broadcasted_iota(jnp.int32, (4, 256), 0)
        == lax.div(lax.broadcasted_iota(jnp.int32, (4, 256), 1), 64)
    ).astype(F32)

    def widen(heads):
        return jnp.dot(heads, lift, preferred_element_type=F32, precision=HIGH)

    raw = widen(accr[...] + rate_bias[...])
    rate = jnp.maximum(raw, 0.0) + jnp.log1p(jnp.exp(-jnp.abs(raw)))
    decay = jnp.exp(rate * -jnp.exp(widen(decay_log[...])))
    skip = widen(skip_gain[...])
    entering = rate * acci[...]
    column = lax.broadcasted_iota(jnp.int32, (256, 1024), 1)
    inside = lax.rem(column, 16)
    owner = lax.div(column, 16)
    spread = (
        (4 * owner + lax.rem(inside, 4) == lax.broadcasted_iota(jnp.int32, (256, 1024), 0))
        & (inside < 12)
    )
    spread = jnp.where(spread, 1.0, 0.0).astype(BF16)

    arrive("ioag")
    io_all = jnp.concatenate([iog[j].astype(F32) for j in range(8)], axis=0)
    in_vec = io_all[:, :256]
    out_vec = io_all[:, 256:]
    wide = jnp.dot(out_vec.astype(BF16), spread, preferred_element_type=F32)
    row_prompt = lax.rem(lax.div(lax.broadcasted_iota(jnp.int32, (192, 1024), 0), 16), 3)
    col_prompt = lax.div(
        lax.rem(lax.broadcasted_iota(jnp.int32, (192, 1024), 1), 16), 4
    )
    wide = jnp.where(row_prompt == col_prompt, wide, 0.0).astype(BF16)
    arrive("st2")
    start = jnp.dot(wide, st2[...].reshape(1024, 256), preferred_element_type=F32)

    mixed = []
    running = None
    carried = []
    for step in range(4):
        rows = slice(48 * step, 48 * step + 48)
        fall = decay[rows]
        running = fall if running is None else running * fall
        carried = [term * fall for term in carried] + [entering[rows]]
        value = running * start[rows]
        for earlier in range(step + 1):
            match = jnp.sum(
                out_vec[rows] * in_vec[48 * earlier : 48 * earlier + 48], axis=1, keepdims=True
            )
            value = value + match * carried[earlier]
        mixed.append(value + skip * acci[rows, :])
    gate = accg[...]
    gated = jnp.concatenate(mixed, axis=0) * (gate / (1.0 + jnp.exp(-gate)))
    gm[:, own_rows] = (gated * mix_gain[...]).astype(BF16)
    swap("gm", gm.at[:, own_rows], gm.at[:, own_rows], sibling)
    sq[i] = row_sums(gated)
    exchange("sq", 8, i, dev_big_x, lambda j: sq.at[i], lambda j: sq.at[j], lambda n: sq.at[pl.ds(0, n)])
    def mix_scale():
        arrive("sq")
        group_sum = sq[0]
        for j in range(1, 8):
            group_sum = group_sum + sq[j]
        return to_column(lax.rsqrt(group_sum * (1.0 / 2048.0) + 1e-05))

    arrive("gm", "loc1", "w0")

    my_rows = pl.ds(al(48 * y, 48), 48)
    low = pl.ds(0, 256)
    high = pl.ds(256, 256)

    def rows_of(j):
        return pl.ds(al(48 * j, 48), 48)

    def half_a(p, c):
        return lambda j, h: p.at[c, pl.ds(2 * h, 2), rows_of(j), low]

    def half_b(p, c):
        return lambda j, h: p.at[c, j, pl.ds(96 * h, 96), high]

    def reduce_scatter(names, left, weight, scaling, p, a1, b1, ja, jb, sa, sb, a2, b2, zs, zr, use):
        na1, nb1, na2, nb2, nz = names
        tails = ("", "x")
        scales = []

        for c in range(2):

            for hh in (1, 0):

                def block(xx, _, c=c, hh=hh):
                    cols = pl.ds(al(1024 * xx + 512 * hh + 256 * c, 256), 256)
                    value = jnp.dot(left[...], weight[:, cols], preferred_element_type=F32)
                    if scaling is not None and c == 0 and hh == 1:
                        plain[xx] = value
                        return 0
                    if scaling is not None:
                        value = value * scales[0]
                    p[c, xx, :, 256 * hh : 256 * hh + 256] = value.astype(BF16)
                    return 0

                lax.fori_loop(0, 4, block, 0, unroll=4)
                if scaling is not None and c == 0 and hh == 1:
                    scales.append(scaling())

                    def rescale(xx, _):
                        p[0, xx, :, 256:512] = (plain[xx] * scales[0]).astype(BF16)
                        return 0

                    lax.fori_loop(0, 4, rescale, 0)
                if hh == 1:
                    ring_start(nb1 + tails[c], x, dev_x, half_b(p, c), b1.at[c])
                else:
                    ring_start(na1 + tails[c], y, dev_y, half_a(p, c), a1.at[c])
        for c in range(2):
            ring_pass(na1 + tails[c], y, dev_y, half_a(p, c), a1.at[c], ja.at[c])
            ring_pass(nb1 + tails[c], x, dev_x, half_b(p, c), b1.at[c], jb.at[c])
        for c in range(2):
            totals = ring_total(na1 + tails[c], y, half_a(p, c), a1.at[c])
            for h in range(2):
                sa[c, 2 * h : 2 * h + 2] = totals[h].astype(BF16)
            exchange(
                na2 + tails[c],
                4,
                x,
                dev_x,
                lambda j, c=c: sa.at[c, j],
                lambda j, c=c: a2.at[c, j],
                lambda n, c=c: a2.at[c, pl.ds(0, n)],
            )
            totals = ring_total(nb1 + tails[c], x, half_b(p, c), b1.at[c])
            for h in range(2):
                sb[c, 96 * h : 96 * h + 96, :] = totals[h].astype(BF16)
            exchange(
                nb2 + tails[c],
                4,
                y,
                dev_y,
                lambda j, c=c: sb.at[c, rows_of(j)],
                lambda j, c=c: b2.at[c, j],
                lambda n, c=c: b2.at[c, pl.ds(0, n)],
            )
        for c in range(2):
            arrive(na2 + tails[c])
            total = sa[c, x].astype(F32)
            for k in range(1, 4):
                total = total + a2[c, lax.rem(x + k, 4)].astype(F32)
            zs[c, :, 0:256] = total.astype(BF16)
            arrive(nb2 + tails[c])
            total = sb[c, my_rows, :].astype(F32)
            for k in range(1, 4):
                total = total + b2[c, lax.rem(y + k, 4)].astype(F32)
            zs[c, :, 256:512] = total.astype(BF16)
            swap(nz + str(c), zs.at[c], zr.at[c], zpeer)
        for c in range(2):
            arrive(nz + str(c))
            use(c, zs[c].astype(F32) + zr[c].astype(F32))

    feature = al(1024 * (4 * t + x), 1024)
    squares = []

    def use_mix(c, value):
        spans = [al(feature + 256 * c, 256), al(feature + 512 + 256 * c, 256)]
        old = jnp.concatenate([hid[my_rows, pl.ds(span, 256)] for span in spans], axis=1)
        gain = jnp.concatenate([gain2[:, pl.ds(span, 256)] for span in spans], axis=1)
        residual = old.astype(F32) + value
        res[c] = residual
        mid[c, x, my_rows, :] = (residual * gain).astype(BF16)
        tail = ("", "x")[c]
        exchange(
            "ma1" + tail,
            4,
            x,
            dev_x,
            lambda j: mid.at[c, x, my_rows, low],
            lambda j: mid.at[c, j, my_rows, low],
            lambda n: mid.at[c, pl.ds(0, n), my_rows, low],
        )
        exchange(
            "mb1" + tail,
            4,
            y,
            dev_y,
            lambda j: mid.at[c, x, my_rows, high],
            lambda j: mid.at[c, x, rows_of(j), high],
            lambda n: mid.at[c, x, pl.ds(0, 48 * n), high],
        )
        squares.append(row_sums(residual))

    reduce_scatter(
        ("a1", "b1", "a2", "b2", "rz"),
        gm,
        wm,
        mix_scale,
        part,
        ra1,
        rb1,
        rja,
        rjb,
        qa,
        qb,
        ra2,
        rb2,
        rzs,
        rzr,
        use_mix,
    )
    sq2[i] = squares[0] + squares[1]
    exchange("sq2", 8, i, dev_big_x, lambda j: sq2.at[i], lambda j: sq2.at[j], lambda n: sq2.at[pl.ds(0, n)])
    for c in range(2):
        tail = ("", "x")[c]
        arrive("ma1" + tail)
        spread_start("ma2" + tail, y, dev_y, half_a(mid, c))
        arrive("mb1" + tail)
        spread_start("mb2" + tail, x, dev_x, half_b(mid, c))
    for c in range(2):
        tail = ("", "x")[c]
        spread_pass(
            "ma2" + tail,
            y,
            dev_y,
            half_a(mid, c),
            lambda n, c=c: mid.at[c, :, pl.ds(0, 48 * n), low],
        )
        spread_pass(
            "mb2" + tail, x, dev_x, half_b(mid, c), lambda n, c=c: mid.at[c, pl.ds(0, n), :, high]
        )
    arrive("sq2")
    row_sum = sq2[0]
    for j in range(1, 8):
        row_sum = row_sum + sq2[j]
    sqy[y] = row_sum
    exchange("sqy", 4, y, dev_y, lambda j: sqy.at[y], lambda j: sqy.at[j], lambda n: sqy.at[pl.ds(0, n)])
    arrive("loc2", "w1", "kvw")
    query = jnp.zeros((192, 256), F32)
    pair = jnp.zeros((192, 256), F32)
    for c in range(2):
        tail = ("", "x")[c]
        for name in ("ma2", "mb2"):
            arrive(name + tail + "g", name + tail + "o")
        if c == 1:
            for xx in range(4):
                pair = pair + jnp.dot(
                    mid[lax.rem(x, 2), xx, :, pl.ds(al(256 * lax.div(x, 2), 256), 256)],
                    kvw[2 * xx : 2 * xx + 2].reshape(256, 256),
                    preferred_element_type=F32,
                )
            arrive("sqy")
            scale = jnp.concatenate(
                [to_column(lax.rsqrt(sqy[j] * (1.0 / 8192.0) + 1e-05)) for j in range(4)], axis=0
            )
            pair = pair * scale
            for j in range(8):
                kvp[j] = pair[24 * j : 24 * j + 24]
            exchange(
                "kvr",
                8,
                i,
                dev_big_x,
                lambda j: kvp.at[j],
                lambda j: kvr.at[j],
                lambda n: kvr.at[pl.ds(0, n)],
            )
        for xx in range(4):
            for hh in range(2):
                place = 1024 * xx + 512 * hh + 256 * c
                query = query + jnp.dot(
                    mid[c, xx, :, 256 * hh : 256 * hh + 256],
                    wq[place : place + 256, :],
                    preferred_element_type=F32,
                )
    qs[...] = query
    swap("q", qs, qr, sibling)

    arrive("kvr")
    pair_sum = kvp[i].astype(F32)
    for k in range(1, 8):
        pair_sum = pair_sum + kvr[lax.rem(i + k, 8)].astype(F32)
    kvg[i] = pair_sum.astype(BF16)
    exchange("kva", 8, i, dev_big_x, lambda j: kvg.at[i], lambda j: kvg.at[j], lambda n: kvg.at[pl.ds(0, n)])

    arrive("q")
    query_rows = ((qs[...] + qr[...]) * (scale * (128.0**-0.5))).astype(BF16)
    arrive("ca2")
    query_of = []
    lane = lax.broadcasted_iota(jnp.int32, (128, 128), 1)
    place = 128 * lax.div(lane, 16) + lax.rem(lane, 16) + 16 * t
    for p in range(3):
        query_p = jnp.concatenate(
            [
                query_rows[48 * step + 16 * p : 48 * step + 16 * p + 16, 128 * head : 128 * head + 128]
                for head in range(2)
                for step in range(4)
            ],
            axis=0,
        )
        query_of.append(query_p)
        for j in range(4):
            keys = ca2[j, p, :, :, 0:128].reshape(128, 128)
            score = nt_dot(query_p, keys)
            scores[p, :, 128 * j : 128 * j + 128] = jnp.where(
                place + 32 * j < lens[p], score, -1e30
            )

    arrive("kva")
    pair_all = jnp.concatenate([kvg[j].astype(F32) for j in range(8)], axis=0)
    row_step = lax.rem(lax.div(lax.broadcasted_iota(jnp.int32, (128, 1), 0), 16), 4)
    row_step = row_step - 4 * t
    wide_lane = lax.broadcasted_iota(jnp.int32, (128, 128), 1)
    for p in range(3):
        far = scores[p]
        top = jnp.max(far, axis=1, keepdims=True)
        near = []
        values = []
        query_p = query_of[p].astype(F32)
        for step in range(4):
            block = pair_all[48 * step + 16 * p : 48 * step + 16 * p + 16]
            tiled = jnp.concatenate([block] * 8, axis=0)
            values.append(tiled[:, 128:])
            score = jnp.sum(query_p * tiled[:, :128], axis=1, keepdims=True)
            score = jnp.where(row_step >= step, score, -1e30)
            near.append(score)
            top = jnp.maximum(top, score)
        far = jnp.exp(far - top)
        near = [jnp.exp(score - top) for score in near]
        total = jnp.sum(far, axis=1, keepdims=True)
        for weight in near:
            total = total + weight
        far = far.astype(BF16)
        result = jnp.zeros((128, 128), F32)
        for j in range(4):
            result = result + jnp.dot(
                far[:, 128 * j : 128 * j + 128],
                ca2[j, p, :, :, 128:256].reshape(128, 128),
                preferred_element_type=F32,
            )
        for weight, value in zip(near, values):
            result = result + weight.astype(BF16).astype(F32) * value
        os[p, :, 0:128] = result
        os[p, :, 128:256] = jnp.where(wide_lane < 64, top, total)
        swap("at" + str(p), os.at[p], orr.at[p], sibling)
    for p in range(3):
        arrive("at" + str(p))
        mine_top, mine_total = os[p, :, 128:129], os[p, :, 192:193]
        peer_top, peer_total = orr[p, :, 128:129], orr[p, :, 192:193]
        top = jnp.maximum(mine_top, peer_top)
        mine = jnp.exp(mine_top - top)
        peer = jnp.exp(peer_top - top)
        total = mine_total * mine + peer_total * peer
        result = (os[p, :, 0:128] * (mine / total) + orr[p, :, 0:128] * (peer / total)).astype(BF16)
        for head in range(2):
            for step in range(4):
                att[48 * step + 16 * p : 48 * step + 16 * p + 16, 128 * head : 128 * head + 128] = (
                    result[64 * head + 16 * step : 64 * head + 16 * step + 16]
                )

    arrive("loc3", "w2")

    def use_out(c, value):
        value = res[c] + value
        fin[0:48, 256 * c : 256 * c + 256] = value[:, 0:256]
        fin[0:48, 512 + 256 * c : 768 + 256 * c] = value[:, 256:512]

    reduce_scatter(
        ("c1", "d1", "c2", "d2", "sz"),
        att,
        wo,
        None,
        part2,
        rc1,
        rd1,
        rjc,
        rjd,
        qc,
        qd,
        rc2,
        rd2,
        szs,
        szr,
        use_out,
    )

    fin[48:56, :] = jnp.zeros((8, 1024), F32)
    sends = lax.div(y, 2) == z

    def fin_copy(k):
        target = 16 * y + k
        return remote(fo.at[k], fi.at[i], "fin", dev(lax.div(target, 2), lax.rem(target, 2)))

    @pl.when(sends)
    def _():
        for k in range(16):
            fo[k] = fin[3 * k : 3 * k + 8, :].astype(BF16)

        def send(k, _):
            @pl.when(16 * y + k == me)
            def _():
                local(fo.at[k], fi.at[i], "fin").start()

            @pl.when(16 * y + k != me)
            def _():
                fin_copy(k).start()

            return 0

        lax.fori_loop(0, 16, send, 0)

    keeps = sends & (lax.div(me, 16) == y)

    def fin_finish():
        @pl.when(keeps)
        def _():
            all_sent(fo.at[pl.ds(0, 15)], "fin")

        @pl.when(sends & (lax.div(me, 16) != y))
        def _():
            all_sent(fo, "fin")

    local(fi, fi, "fin").wait()
    finish.append(fin_finish)
    for j in range(8):
        place_j = 1024 * (4 * (j % 2) + j // 2)
        out[:, place_j : place_j + 1024] = fi[j][0:3, :]
    drain()


def scratch():
    def v(shape, dtype=BF16):
        return pltpu.VMEM(shape, dtype)

    reduce_bufs = [
        v((2, 6, 2, 48, 256)),
        v((2, 6, 96, 256)),
        v((2, 2, 2, 48, 256)),
        v((2, 2, 96, 256)),
        v((2, 4, 48, 256)),
        v((2, 192, 256)),
        v((2, 4, 48, 256)),
        v((2, 4, 48, 256)),
        v((2, 48, 512)),
        v((2, 48, 512)),
    ]
    return [
        v((192, 8192)),
        v((192, 8192)),
        v((8192, 256)),
        v((8192, 256)),
        v((512, 4096)),
        v((4096, 256)),
        v((256, 4096)),
        v((8, 128, 512)),
        v((8, 128, 256)),
        v((8, 8, 16, 256)),
        v((8, 8, 16, 256)),
        v((3, 8, 16, 256)),
        v((4, 3, 8, 16, 256)),
        v((192, 256), F32),
        v((192, 256), F32),
        v((192, 4), F32),
        v((192, 1024)),
        v((8, 24, 512), F32),
        v((8, 24, 512), F32),
        v((8, 24, 512)),
        v((8, 8, 192), F32),
        v((192, 512)),
        v((2, 4, 192, 512)),
        *reduce_bufs,
        v((2, 48, 512), F32),
        v((8, 8, 48), F32),
        v((4, 8, 48), F32),
        v((2, 4, 192, 512)),
        v((192, 256), F32),
        v((192, 256), F32),
        v((8, 24, 256), F32),
        v((8, 24, 256), F32),
        v((8, 24, 256)),
        v((3, 128, 512), F32),
        v((3, 128, 256), F32),
        v((3, 128, 256), F32),
        v((192, 256)),
        v((2, 4, 192, 512)),
        *reduce_bufs,
        v((56, 1024), F32),
        v((16, 8, 1024)),
        v((8, 8, 1024)),
        v((4, 192, 256), F32),
        v((3, 64, 4, 256), F32),
        v((2, 1024, 128), F32),
        v((8, 8, 16, 256)),
        v((3, 16, 8, 256)),
        v((2, 384, 128), F32),
        v((8, 3, 16, 256)),
        pltpu.SemaphoreType.DMA((SENDS,)),
        pltpu.SemaphoreType.DMA((LANDINGS,)),
        pltpu.SemaphoreType.DMA((8,)),
    ]


def shards(
    hidden_input,
    prompt_lengths,
    prompt_states,
    prompt_cache,
    input_gain,
    gate_weight,
    input_weight,
    rate_weight,
    rate_bias,
    decay_log,
    skip_gain,
    state_io_weight,
    mix_gain,
    mix_weight,
    middle_gain,
    query_weight,
    key_value_weight,
    output_weight,
):
    hidden = hidden_input.reshape(192, 8192)
    states = prompt_states.transpose(0, 2, 3, 1)
    vmem = pl.BlockSpec(memory_space=pltpu.VMEM)
    smem = pl.BlockSpec(memory_space=pltpu.SMEM)
    anyw = pl.BlockSpec(memory_space=pl.ANY)
    return pl.pallas_call(
        kernel,
        out_shape=jax.ShapeDtypeStruct((3, 8192), BF16),
        in_specs=[
            smem,
            anyw,
            anyw,
            anyw,
            vmem,
            anyw,
            anyw,
            vmem,
            vmem,
            vmem,
            vmem,
            vmem,
            anyw,
            anyw,
            vmem,
            anyw,
            anyw,
            anyw,
        ],
        out_specs=vmem,
        scratch_shapes=scratch(),
        compiler_params=pltpu.CompilerParams(
            collective_id=0, has_side_effects=True, vmem_limit_bytes=60 * 1024 * 1024
        ),
        cost_estimate=pl.CostEstimate(
            flops=4_000_000_000, bytes_accessed=24_000_000, transcendentals=1_000_000
        ),
    )(
        prompt_lengths,
        hidden,
        states,
        prompt_cache,
        input_gain[None, :],
        gate_weight,
        input_weight,
        rate_weight.T,
        rate_bias[None, :],
        decay_log[None, :],
        skip_gain[None, :],
        mix_gain[None, :],
        state_io_weight,
        mix_weight,
        middle_gain[None, :],
        query_weight,
        key_value_weight,
        output_weight,
    )


def solution(mesh):
    in_specs = (
        P(None, "prompt", None),
        P("prompt"),
        P("prompt", None, None, ("sample", "tensor")),
        P("prompt", ("sample", "tensor"), None, None),
        P(),
        P(None, ("sample", "tensor")),
        P(None, ("sample", "tensor")),
        P(None, ("sample", "tensor")),
        P(("sample", "tensor")),
        P(("sample", "tensor")),
        P(("sample", "tensor")),
        P(("sample", "tensor"), None),
        P(("sample", "tensor")),
        P(("sample", "tensor"), None),
        P(),
        P(None, ("sample", "tensor")),
        P(("sample", "tensor"), None),
        P(("sample", "tensor"), None),
    )
    out_specs = P(("prompt", "sample", "tensor"), None)
    return jax.shard_map(shards, mesh=mesh, in_specs=in_specs, out_specs=out_specs, check_vma=False)
```
